128 devices in a mesh: row: 16 (over y, x_hi, core), rep: 8 (over x_lo, z).
Axes of the slice: x: 4 (x_hi: 2, x_lo: 2; x = x_hi * 2 + x_lo), y: 4, z: 4, core: 2. Of those that a mesh axis runs over, the one named last changes fastest.
Arguments:
- features: float32 [32768, 256], P('row'), may hold values from -6 to 6
- adjacency_tiles: float32 [16, 8, 256, 128, 128], P('row', 'rep'), may hold values from -0.25 to 0.25
- tile_rows: int32 [16, 8, 256], P('row', 'rep'), may hold values from 0 to 15, as said below
- tile_cols: int32 [16, 8, 256], P('row', 'rep'), may hold values from 0 to 31, as said below
- tile_counts: int32 [16, 8], P('row', 'rep'), may hold values from 32 to 256, as said below
- plan: int32 [8, 2], replicated, may hold values from 0 to 15, as said below
- weights: float32 [2, 256, 256], replicated, may hold values from -0.375 to 0.375
Outputs:
- embedded: float32 [32768, 256], P(('row', 'rep'))
The draws below stay inside these ranges and needn't reach their ends.
Inputs may be any that keep to these rules, and one draw needn't show every extreme that they name: Within one block row and replica the listed positions (tile_rows, tile_cols) are distinct. Within one block row and replica the listed positions (tile_rows, tile_cols) are distinct. `tile_counts`: some block row and replica lists exactly 256 tiles. `plan`: every block row 0 to 15 appears exactly once in the table.
All inputs are finite; a program needn't handle non-finite values.
Results may differ from the reference program's by a relative error of at most 0.0003.
Values sent between devices are 32-bit elements; how exact they have to be, the bound alone decides.
A program may use at most 128 MiB of HBM per device.

```python
import jax
import jax.numpy as jnp
from jax import lax

F = 256
TILE = 128
LAYERS = 2
VB = 2048
SECTIONS = 2
TMAX = 256
NV = 32768
N_ROW = 16
N_REP = 8


def tile_positions(key):
    row_tiles = VB // TILE
    position_count = SECTIONS * row_tiles * row_tiles
    device_keys = jax.random.split(jax.random.fold_in(key, 17), N_ROW * N_REP)

    def pick_one(device_key):
        return jax.random.permutation(device_key, position_count)[:TMAX]
    chosen = jax.vmap(pick_one)(device_keys).reshape(N_ROW, N_REP, TMAX).astype(jnp.int32)
    return (chosen % row_tiles, chosen // row_tiles)


def draw_tile_rows(key, part):
    return tile_positions(key)[0]


def draw_tile_cols(key, part):
    return tile_positions(key)[1]


def draw_tile_counts(key, part):
    factors = jax.random.randint(jax.random.fold_in(key, 31), (3, N_ROW, N_REP), 0, 9)
    combined = factors[0] * factors[1] * factors[2]
    lowest = TMAX // 8
    counted = lowest + (TMAX - lowest) * combined // 512
    flat_counts = counted.reshape(N_ROW * N_REP)
    picked = jax.random.randint(jax.random.fold_in(key, 37), (), 0, N_ROW * N_REP)
    positions = jnp.arange(N_ROW * N_REP, dtype=jnp.int32)
    flat_counts = jnp.where(positions == picked, TMAX, flat_counts)
    return flat_counts.reshape(N_ROW, N_REP).astype(jnp.int32)


def draw_plan(key, part):
    order_ids = jax.random.permutation(jax.random.fold_in(key, 23), N_ROW)
    return order_ids.reshape(N_REP, SECTIONS).astype(jnp.int32)


def block_levels(own_key, dims, cuts, low, high):
    def one(axis_at, shards_of):
        heights = jax.random.uniform(jax.random.fold_in(jax.random.fold_in(own_key, 6), axis_at), (shards_of,), jnp.float32, low / len(cuts), high / len(cuts))
        return jnp.repeat(jnp.exp(heights), dims[axis_at] // shards_of).reshape((-1,) + (1,) * (len(dims) - axis_at - 1))

    factor_of = one(*cuts[0])
    for cut in cuts[1:]:
        factor_of = factor_of * one(*cut)
    return factor_of


def gaussian(rng, dims, width, most, cuts=(), held_as=jnp.bfloat16):
    result = width * jax.random.normal(rng, dims, jnp.float32)
    if cuts:
        result = result * block_levels(rng, dims, cuts, -0.22, 0.18)
    return jnp.clip(result, -most, most).astype(held_as)


def setup_inputs(seed: int = 0) -> dict:
    streams_of = jax.random.split(jax.random.key(seed), 8)
    return {
        "features": gaussian(streams_of[0], (NV, F), 1.0, 6.0, ((0, 16),), jnp.float32),
        "adjacency_tiles": gaussian(streams_of[1], (N_ROW, N_REP, TMAX, TILE, TILE), (TILE * TMAX // (4 * (VB // TILE))) ** -0.5, 0.25, ((0, 16), (1, 8)), jnp.float32),
        "tile_rows": draw_tile_rows(jax.random.fold_in(streams_of[7], 71), 0),
        "tile_cols": draw_tile_cols(jax.random.fold_in(streams_of[7], 71), 0),
        "tile_counts": draw_tile_counts(jax.random.fold_in(streams_of[7], 71), 0),
        "plan": draw_plan(jax.random.fold_in(streams_of[7], 71), 0),
        "weights": gaussian(streams_of[6], (LAYERS, F, F), F ** -0.5, 0.375, (), jnp.float32),
    }


def spread(hidden, adjacency_tiles, tile_rows, tile_cols, tile_counts, plan):
    row_tiles = VB // TILE
    pieces = hidden.reshape(N_ROW * row_tiles, TILE, F)
    slot_ids = jnp.arange(TMAX, dtype=jnp.int32)
    lane_ids = jnp.arange(row_tiles, dtype=jnp.int32)

    def one_row(row_num):
        def one_rep(running, rep_num):
            column_ids = tile_cols[row_num, rep_num]
            owner_ids = plan[rep_num][column_ids // row_tiles]
            picked = (owner_ids * row_tiles + column_ids % row_tiles).astype(jnp.int32)
            sources = jnp.take(pieces, picked, axis=0)
            live_mask = (slot_ids < tile_counts[row_num, rep_num]).astype(jnp.float32)
            product = jnp.einsum("tij,tjf->tif", adjacency_tiles[row_num, rep_num], sources, precision=lax.Precision.HIGHEST)
            product = product * live_mask[:, None, None]
            placing = (tile_rows[row_num, rep_num][None, :] == lane_ids[:, None]).astype(jnp.float32)
            added = jnp.dot(placing, product.reshape(TMAX, TILE * F), precision=lax.Precision.HIGHEST)
            return running + added, None

        start = jnp.zeros((row_tiles, TILE * F), jnp.float32)
        running, unused = lax.scan(one_rep, start, jnp.arange(N_REP, dtype=jnp.int32))
        return running.reshape(VB, F)

    return lax.map(one_row, jnp.arange(N_ROW, dtype=jnp.int32)).reshape(NV, F)


def reference(features, adjacency_tiles, tile_rows, tile_cols, tile_counts, plan, weights):
    hidden = features
    for layer_num in range(LAYERS):
        aggregated = spread(hidden, adjacency_tiles, tile_rows, tile_cols, tile_counts, plan)
        hidden = jnp.maximum(jnp.dot(aggregated, weights[layer_num], precision=lax.Precision.HIGHEST), 0.0)
    return hidden
```

```python
import functools

import jax
import jax.numpy as jnp
from jax import lax
from jax.experimental import pallas as pl
from jax.experimental.pallas import tpu as pltpu
from jax.sharding import PartitionSpec as P

BF = jnp.bfloat16
F32 = jnp.float32
MESH = pl.DeviceIdType.MESH
Y, XH, C, XL, Z = 4, 2, 2, 2, 4
GROUP = 16
STAGES = 4
COPIES = 160


def mm(a, b):
    return jnp.dot(a, b, preferred_element_type=F32)


def split(v):
    high = v.astype(BF)
    return high, (v - high.astype(F32)).astype(BF)


def kernel(
    pos, plan, x_ref, tiles, w_ref, o_ref,
    stage, hi, lo, land, acc, acc_out, buf_00, buf_01, buf_10, buf_11, send_b, hid, bh, bl,
    r1, r2, q1, q3, r3, f1, f2, g1, g3, f3,
    stage_sem, ssem, rsem, a_send, a_recv, b_send, b_recv,
):
    row, rep = lax.axis_index("row"), lax.axis_index("rep")
    y, xh, c = row // 4, (row // 2) % 2, row % 2
    xl, z = rep // 4, rep % 4

    def rows_dev(dy, dx, dc):
        return ((y + dy) % 4) * 4 + ((xh + dx) % 2) * 2 + (c + dc) % 2

    def reps_dev(dx, dz):
        return ((xl + dx) % 2) * 4 + (z + dz) % 4

    row_peers = [
        rows_dev(a, b, d) for a in range(4) for b in range(2) for d in range(2) if (a, b, d) != (0, 0, 0)
    ]
    rep_peers = [reps_dev(a, b) for a in range(2) for b in range(4) if (a, b) != (0, 0)]

    def load_tiles(g, slot):
        return pltpu.make_async_copy(
            tiles.at[pl.ds(g * GROUP, GROUP)], stage.at[slot], stage_sem.at[slot]
        )

    for g in range(STAGES):
        load_tiles(g, g).start()

    barrier = pltpu.get_barrier_semaphore()
    for peer in row_peers:
        pl.semaphore_signal(barrier, inc=1, device_id=(peer, rep), device_id_type=MESH)
    for peer in rep_peers:
        pl.semaphore_signal(barrier, inc=1, device_id=(row, peer), device_id_type=MESH)
    pl.semaphore_wait(barrier, 22)

    used = [0]
    sent = []

    def remote(src, dst, dev):
        n = used[0]
        used[0] += 1
        copy = pltpu.make_async_remote_copy(
            src_ref=src, dst_ref=dst, send_sem=ssem.at[n], recv_sem=rsem.at[n],
            device_id=dev, device_id_type=MESH,
        )
        sent.append(copy)
        copy.start()
        return copy

    buf_a = ((buf_00, buf_01), (buf_10, buf_11))

    def send_a(layer, h, source):
        for peer in row_peers:
            pltpu.make_async_remote_copy(
                src_ref=source(peer), dst_ref=buf_a[layer][h].at[row],
                send_sem=a_send.at[layer, h], recv_sem=a_recv.at[layer, h],
                device_id=(peer, rep), device_id_type=MESH,
            ).start()
        pltpu.make_async_copy(source(row), buf_a[layer][h].at[row], a_recv.at[layer, h]).start()

    def turn(layer, h):
        whole = buf_a[layer][h]
        pltpu.make_async_copy(whole, whole, a_recv.at[layer, h]).wait()
        for k in range(8):
            for s in range(2):
                send_b[layer, h, k, s] = buf_a[layer][h][plan[k * 2 + s]]
        for peer in rep_peers:
            pltpu.make_async_remote_copy(
                src_ref=send_b.at[layer, h, peer], dst_ref=land.at[layer, :, h, row, rep],
                send_sem=b_send.at[layer, h], recv_sem=b_recv.at[layer, h],
                device_id=(row, peer), device_id_type=MESH,
            ).start()
        pltpu.make_async_copy(
            send_b.at[layer, h, rep], land.at[layer, :, h, row, rep], b_recv.at[layer, h]
        ).start()

    def wait_b(layer, h):
        mine = land.at[layer, :, h, row]
        pltpu.make_async_copy(mine, mine, b_recv.at[layer, h]).wait()

    def convert(first, last):
        def one(g, carry):
            slot = lax.rem(g, STAGES)
            load_tiles(g, slot).wait()

            def tile(t, inner):
                high, low = split(stage[slot, t])
                hi[g * GROUP + t] = high
                lo[g * GROUP + t] = low
                return inner

            lax.fori_loop(0, GROUP, tile, 0, unroll=4)

            @pl.when(g + STAGES < 256 // GROUP)
            def _():
                load_tiles(g + STAGES, slot).start()

            return carry

        lax.fori_loop(first, last, one, 0)

    def products(layer, h, yy, out, row_tiles, whole=True):
        def one(j, carry):
            q = yy * 2 + j
            t = h * 8 + q
            f0 = land[layer, 0, h, pl.ds(q * 2, 2)].reshape(128, 256)
            f1_ = land[layer, 1, h, pl.ds(q * 2, 2)].reshape(128, 256)
            bh[0:128], bl[0:128] = split(f0)
            bh[128:256], bl[128:256] = split(f1_)
            for i in row_tiles:
                a0, a1 = pos[i * 32 + t], pos[i * 32 + 16 + t]
                top = jnp.concatenate([hi[a0], hi[a1]], axis=1)
                low = jnp.concatenate([lo[a0], lo[a1]], axis=1)
                added = mm(top, bh[...]) + mm(top, bl[...]) + mm(low, bh[...])
                out[2 * i : 2 * i + 2] += added.reshape(2, 8, 8, 256)
            return carry

        lax.fori_loop(0, 2, one, 0)

    class Gather:
        def __init__(self, layer, h):
            self.l, self.h = layer, h

        def piece(self, yy, xx, cc):
            return land.at[self.l, :, self.h, (yy % 4) * 4 + (xx % 2) * 2 + cc]

        def half(self, s, yy, xx, cc):
            return land.at[self.l, s, self.h, (yy % 4) * 4 + (xx % 2) * 2 + cc]

        def move(self, ref, dy, dx, dc):
            return remote(ref, ref, (rows_dev(dy, dx, dc), rep))

        def own(self):
            mine = self.piece(y, xh, c)
            self.x = self.move(mine, 0, 1, 0)
            self.up = [self.move(mine, 1, 0, 0), None]
            self.down = [self.move(mine, 3, 0, 0), None]
            self.core = {"y": [self.move(mine, 0, 0, 1)]}

        def partner(self):
            self.x.wait_recv()
            got = self.piece(y, xh + 1, c)
            self.up[1] = self.move(got, 1, 0, 0)
            self.down[1] = self.move(got, 3, 0, 0)
            self.core["y"].append(self.move(got, 0, 0, 1))

        def pass_on(self, n):
            self.up[n].wait_recv()
            up2 = self.move(self.half(0, y + 3, xh + n, c), 1, 0, 0)
            to_core = self.move(self.piece(y + 3, xh + n, c), 0, 0, 1)
            self.core.setdefault("m", []).append(to_core)
            self.down[n].wait_recv()
            down2 = self.move(self.half(1, y + 1, xh + n, c), 3, 0, 0)
            to_core = self.move(self.piece(y + 1, xh + n, c), 0, 0, 1)
            self.core.setdefault("p", []).append(to_core)
            self.core.setdefault("far", []).append((up2, down2))

        def far(self, n):
            up2, down2 = self.core["far"][n]
            up2.wait_recv()
            a = self.move(self.half(0, y + 2, xh + n, c), 0, 0, 1)
            down2.wait_recv()
            b = self.move(self.half(1, y + 2, xh + n, c), 0, 0, 1)
            self.core.setdefault("f", []).extend([a, b])

        def ready(self, name):
            for copy in self.core[name]:
                copy.wait_recv()

    def gather_and_multiply(layer, out, first_rows, rest_rows, begin_sum):
        every = range(16)
        a, b = Gather(layer, 0), Gather(layer, 1)
        wait_b(layer, 0)
        a.own()
        yield
        wait_b(layer, 1)
        b.own()
        a.partner()
        a.pass_on(0)
        b.partner()
        a.ready("y")
        products(layer, 0, y, out, every)
        a.pass_on(1)
        b.pass_on(0)
        a.ready("m")
        products(layer, 0, (y + 3) % 4, out, every)
        a.far(0)
        b.pass_on(1)
        a.ready("p")
        products(layer, 0, (y + 1) % 4, out, every)
        a.far(1)
        b.far(0)
        a.ready("f")
        products(layer, 0, (y + 2) % 4, out, every)
        b.far(1)
        b.ready("y")
        products(layer, 1, y, out, every)
        b.ready("m")
        products(layer, 1, (y + 3) % 4, out, every)
        b.ready("p")
        b.ready("f")
        products(layer, 1, (y + 1) % 4, out, first_rows)
        products(layer, 1, (y + 2) % 4, out, first_rows)
        begin_sum()
        products(layer, 1, (y + 1) % 4, out, rest_rows)
        products(layer, 1, (y + 2) % 4, out, rest_rows)

    class Reduce:
        def __init__(self, h, part, r1, r2, q1, q3, r3):
            self.h, self.part = h, part
            self.r1, self.r2, self.q1, self.q3, self.r3 = (
                r1.at[h], r2.at[h], q1.at[h], q3.at[h], r3.at[h]
            )

        def start(self):
            up, down = (row, reps_dev(0, 1)), (row, reps_dev(0, 3))
            self.raw = [
                remote(self.part(reps_dev(0, 2) % 4), self.r1.at[0], up),
                remote(self.part(4 + reps_dev(0, 2) % 4), self.r1.at[1], down),
            ]
            zu, zd = (z + 1) % 4, (z + 3) % 4
            self.second = [
                remote(self.part(4 + zu), self.r2.at[0, 1], up),
                remote(self.part(zd), self.r2.at[1, 0], down),
            ]

        def pass_on(self):
            up, down = (row, reps_dev(0, 1)), (row, reps_dev(0, 3))
            zu, zd = (z + 1) % 4, (z + 3) % 4
            self.raw[0].wait_recv()
            self.q1[0] = self.part(zu)[...] + self.r1[0]
            self.second.append(remote(self.q1.at[0], self.r2.at[0, 0], up))
            self.raw[1].wait_recv()
            self.q1[1] = self.part(4 + zd)[...] + self.r1[1]
            self.second.append(remote(self.q1.at[1], self.r2.at[1, 1], down))

        def cross(self):
            for copy in self.second:
                copy.wait_recv()
            other = 1 - xl
            self.q3[...] = self.part(other * 4 + z)[...] + self.r2[0, other] + self.r2[1, other]
            self.last = remote(self.q3, self.r3, (row, reps_dev(1, 0)))

        def finish(self, layer):
            mine = self.part(rep)[...] + self.r2[0, xl] + self.r2[1, xl]
            self.last.wait_recv()
            total = (mine + self.r3[...]).reshape(128, 256)
            wh, wl = split(w_ref[layer])
            th, tl = split(total)
            return jnp.maximum(mm(th, wh) + mm(th, wl) + mm(tl, wh), 0.0)

    for h in range(2):
        send_a(0, h, lambda p: x_ref.at[h, p, rep])
    hi[256] = jnp.zeros((128, 128), BF)
    lo[256] = jnp.zeros((128, 128), BF)

    def clear(i, carry):
        acc[i] = jnp.zeros((8, 8, 256), F32)
        acc_out[i] = jnp.zeros((8, 8, 256), F32)
        return carry

    lax.fori_loop(0, 32, clear, 0)
    convert(0, 6)
    turn(0, 0)
    turn(0, 1)
    convert(6, 256 // GROUP)

    mid = [
        Reduce(h, lambda k, h=h: acc.at[pl.ds(16 * h, 16), k], r1, r2, q1, q3, r3) for h in range(2)
    ]
    for _ in gather_and_multiply(0, acc, range(8), range(8, 16), mid[0].start):
        pass
    mid[1].start()
    mid[0].pass_on()
    mid[0].cross()
    mid[1].pass_on()
    hid[0] = mid[0].finish(0).reshape(16, 8, 256)
    send_a(1, 0, lambda p: hid.at[0, p])
    turn(1, 0)
    mid[1].cross()
    step = gather_and_multiply(
        1, acc_out, range(0, 16, 2), range(1, 16, 2), lambda: end[0].start()
    )
    end = [
        Reduce(h, lambda k, h=h: acc_out.at[pl.ds(4 * k + 2 * h, 2)], f1, f2, g1, g3, f3) for h in range(2)
    ]
    next(step)
    hid[1] = mid[1].finish(0).reshape(16, 8, 256)
    send_a(1, 1, lambda p: hid.at[1, p])
    turn(1, 1)
    for _ in step:
        pass
    end[1].start()
    end[0].pass_on()
    end[1].pass_on()
    end[0].cross()
    end[1].cross()
    o_ref[0:128] = end[0].finish(1)
    o_ref[128:256] = end[1].finish(1)

    for copy in sent:
        copy.wait_send()
    for layer in range(2):
        for h in range(2):
            some = buf_a[layer][h].at[0:15]
            pltpu.make_async_copy(some, some, a_send.at[layer, h]).wait()
            some = send_b.at[layer, h, 0:7]
            pltpu.make_async_copy(some, some, b_send.at[layer, h]).wait()


def shards(features, adjacency_tiles, tile_rows, tile_cols, tile_counts, plan, weights):
    rows, cols, count = tile_rows[0, 0], tile_cols[0, 0], tile_counts[0, 0]
    slots = jnp.arange(256, dtype=jnp.int32)
    place = jnp.where(slots < count, rows * 32 + cols, -1)
    spots = jnp.arange(512, dtype=jnp.int32)
    pos = jnp.min(jnp.where(place[None, :] == spots[:, None], slots[None, :], 256), axis=1)
    piece = (2, 16, 8, 256)
    flat = (2, 2, 8, 8, 256)
    dma = pltpu.SemaphoreType.DMA
    return pl.pallas_call(
        kernel,
        name="graph_layers",
        out_shape=jax.ShapeDtypeStruct((256, 256), F32),
        in_specs=[
            pl.BlockSpec(memory_space=pltpu.SMEM),
            pl.BlockSpec(memory_space=pltpu.SMEM),
            pl.BlockSpec(memory_space=pl.ANY),
            pl.BlockSpec(memory_space=pl.ANY),
            pl.BlockSpec(memory_space=pltpu.VMEM),
        ],
        out_specs=pl.BlockSpec(memory_space=pltpu.VMEM),
        scratch_shapes=[
            pltpu.VMEM((STAGES, GROUP, 128, 128), F32),
            pltpu.VMEM((257, 128, 128), BF),
            pltpu.VMEM((257, 128, 128), BF),
            pltpu.VMEM((2, 2, 2, 16, 8, 8, 256), F32),
            pltpu.VMEM((32, 8, 8, 256), F32),
            pltpu.VMEM((32, 8, 8, 256), F32),
            pltpu.VMEM((16, 8, 256), F32),
            pltpu.VMEM((16, 8, 256), F32),
            pltpu.VMEM((16, 8, 256), F32),
            pltpu.VMEM((16, 8, 256), F32),
            pltpu.VMEM((2, 2, 8, 2, 8, 256), F32),
            pltpu.VMEM((2, 16, 8, 256), F32),
            pltpu.VMEM((256, 256), BF),
            pltpu.VMEM((256, 256), BF),
            pltpu.VMEM((2,) + piece, F32),
            pltpu.VMEM((2, 2) + piece, F32),
            pltpu.VMEM((2,) + piece, F32),
            pltpu.VMEM((2, 16, 8, 256), F32),
            pltpu.VMEM((2, 16, 8, 256), F32),
            pltpu.VMEM((2,) + flat, F32),
            pltpu.VMEM((2, 2) + flat, F32),
            pltpu.VMEM((2,) + flat, F32),
            pltpu.VMEM((2, 2, 8, 8, 256), F32),
            pltpu.VMEM((2, 2, 8, 8, 256), F32),
            dma((STAGES,)),
            dma((COPIES,)),
            dma((COPIES,)),
            dma((2, 2)),
            dma((2, 2)),
            dma((2, 2)),
            dma((2, 2)),
        ],
        compiler_params=pltpu.CompilerParams(
            collective_id=0, has_side_effects=True, vmem_limit_bytes=58 * 2**20
        ),
    )(
        pos,
        plan.reshape(16),
        features.reshape(2, 16, 8, 8, 256),
        adjacency_tiles.reshape(256, 128, 128),
        weights,
    )


def solution(mesh):
    return jax.shard_map(
        shards,
        mesh=mesh,
        in_specs=(
            P("row", None),
            P("row", "rep", None, None, None),
            P("row", "rep", None),
            P("row", "rep", None),
            P("row", "rep"),
            P(),
            P(),
        ),
        out_specs=P(("row", "rep"), None),
        check_vma=False,
    )
```

```python
import functools

import jax
import jax.numpy as jnp
from jax import lax
from jax.experimental import pallas as pl
from jax.experimental.pallas import tpu as pltpu
from jax.sharding import PartitionSpec as P

BF = jnp.bfloat16
F32 = jnp.float32
MESH = pl.DeviceIdType.MESH
Y, XH, C, XL, Z = 4, 2, 2, 2, 4
GROUP = 16
STAGES = 4
COPIES = 160


def mm(a, b):
    return jnp.dot(a, b, preferred_element_type=F32)


def split(v):
    high = v.astype(BF)
    return high, (v - high.astype(F32)).astype(BF)


def kernel(
    pos, plan, x_ref, tiles, w_ref, o_ref,
    stage, hi, lo, land, acc, acc_out, buf_00, buf_01, buf_10, buf_11, send_b, hid, bh, bl,
    mx, mx_made, mz, mz_made, ex, ex_made, ez, ez_made,
    stage_sem, ssem, rsem, a_send, a_recv, b_send, b_recv,
):
    row, rep = lax.axis_index("row"), lax.axis_index("rep")
    y, xh, c = row // 4, (row // 2) % 2, row % 2
    xl, z = rep // 4, rep % 4

    def rows_dev(dy, dx, dc):
        return ((y + dy) % 4) * 4 + ((xh + dx) % 2) * 2 + (c + dc) % 2

    def reps_dev(dx, dz):
        return ((xl + dx) % 2) * 4 + (z + dz) % 4

    row_peers = [
        rows_dev(a, b, d) for a in range(4) for b in range(2) for d in range(2) if (a, b, d) != (0, 0, 0)
    ]
    rep_peers = [reps_dev(a, b) for a in range(2) for b in range(4) if (a, b) != (0, 0)]

    def load_tiles(g, slot):
        return pltpu.make_async_copy(
            tiles.at[pl.ds(g * GROUP, GROUP)], stage.at[slot], stage_sem.at[slot]
        )

    for g in range(STAGES):
        load_tiles(g, g).start()

    barrier = pltpu.get_barrier_semaphore()
    for peer in row_peers:
        pl.semaphore_signal(barrier, inc=1, device_id=(peer, rep), device_id_type=MESH)
    for peer in rep_peers:
        pl.semaphore_signal(barrier, inc=1, device_id=(row, peer), device_id_type=MESH)
    pl.semaphore_wait(barrier, 22)

    used = [0]
    sent = []

    def remote(src, dst, dev):
        n = used[0]
        used[0] += 1
        copy = pltpu.make_async_remote_copy(
            src_ref=src, dst_ref=dst, send_sem=ssem.at[n], recv_sem=rsem.at[n],
            device_id=dev, device_id_type=MESH,
        )
        sent.append(copy)
        copy.start()
        return copy

    buf_a = ((buf_00, buf_01), (buf_10, buf_11))

    def send_a(layer, h, source):
        for peer in row_peers:
            pltpu.make_async_remote_copy(
                src_ref=source(peer), dst_ref=buf_a[layer][h].at[row],
                send_sem=a_send.at[layer, h], recv_sem=a_recv.at[layer, h],
                device_id=(peer, rep), device_id_type=MESH,
            ).start()
        pltpu.make_async_copy(source(row), buf_a[layer][h].at[row], a_recv.at[layer, h]).start()

    def turn(layer, h):
        whole = buf_a[layer][h]
        pltpu.make_async_copy(whole, whole, a_recv.at[layer, h]).wait()
        for k in range(8):
            for s in range(2):
                send_b[layer, h, k, s] = buf_a[layer][h][plan[k, s]]
        for peer in rep_peers:
            pltpu.make_async_remote_copy(
                src_ref=send_b.at[layer, h, peer], dst_ref=land.at[layer, :, h, row, rep],
                send_sem=b_send.at[layer, h], recv_sem=b_recv.at[layer, h],
                device_id=(row, peer), device_id_type=MESH,
            ).start()
        pltpu.make_async_copy(
            send_b.at[layer, h, rep], land.at[layer, :, h, row, rep], b_recv.at[layer, h]
        ).start()

    def wait_b(layer, h):
        mine = land.at[layer, :, h, row]
        pltpu.make_async_copy(mine, mine, b_recv.at[layer, h]).wait()

    def convert(first, last):
        def one(g, carry):
            slot = lax.rem(g, STAGES)
            load_tiles(g, slot).wait()

            def tile(t, inner):
                high, low = split(stage[slot, t])
                hi[g * GROUP + t] = high
                lo[g * GROUP + t] = low
                return inner

            lax.fori_loop(0, GROUP, tile, 0, unroll=4)

            @pl.when(g + STAGES < 256 // GROUP)
            def _():
                load_tiles(g + STAGES, slot).start()

            return carry

        lax.fori_loop(first, last, one, 0)

    def products(layer, tile_of, count, out, row_tiles):
        def one(j, carry):
            h, q = tile_of(j)
            t = h * 8 + q
            f0 = land[layer, 0, h, pl.ds(q * 2, 2)].reshape(128, 256)
            f1_ = land[layer, 1, h, pl.ds(q * 2, 2)].reshape(128, 256)
            bh[0:128], bl[0:128] = split(f0)
            bh[128:256], bl[128:256] = split(f1_)
            for i in row_tiles:
                a0, a1 = pos[i * 32 + t], pos[i * 32 + 16 + t]
                top = jnp.concatenate([hi[a0], hi[a1]], axis=1)
                low = jnp.concatenate([lo[a0], lo[a1]], axis=1)
                added = mm(top, bh[...]) + mm(top, bl[...]) + mm(low, bh[...])
                out[2 * i : 2 * i + 2] += added.reshape(2, 8, 8, 256)
            return carry

        lax.fori_loop(0, count, one, 0)

    def chip(dy, dx):
        return ((y + dy) % 4) * 2 + (xh + dx) % 2

    def gather_and_multiply(layer, out, rows_of, begin):
        every = range(16)
        core = {}

        def piece(h, dy, dx):
            return land.at[layer, :, h, chip(dy, dx) * 2 + c]

        def half(h, s, dy, dx):
            return land.at[layer, s, h, chip(dy, dx) * 2 + c]

        def move(ref, dy, dx, dc):
            return remote(ref, ref, (rows_dev(dy, dx, dc), rep))

        def share(h, dy, dx):
            core.setdefault((h, dy, dx), []).append(move(piece(h, dy, dx), 0, 0, 1))

        def ready(*keys):
            for key in keys:
                for copy in core[key]:
                    copy.wait_recv()

        def both_ways(h, dx):
            mine = piece(h, 0, dx)
            return move(mine, 1, 0, 0), move(mine, 3, 0, 0)

        far, crossed = {}, {}

        def cross(h, dy):
            crossed[h, dy] = move(piece(h, dy, 0), 0, 1, 0)

        def pass_on(h, dx, pair):
            pair[0].wait_recv()
            a = move(half(h, 0, 3, dx), 1, 0, 0)
            share(h, 3, dx)
            if h == 1:
                cross(h, 3)
            pair[1].wait_recv()
            b = move(half(h, 1, 1, dx), 3, 0, 0)
            share(h, 1, dx)
            if h == 1:
                cross(h, 1)
            far[h, dx] = (a, b)

        def end_far(h, dx):
            for copy in far[h, dx]:
                copy.wait_recv()
            share(h, 2, dx)
            if h == 1:
                cross(h, 2)

        def end_cross(dy):
            crossed[1, dy].wait_recv()
            share(1, dy, 1)

        wait_b(layer, 1)
        along1 = both_ways(1, 0)
        share(1, 0, 0)
        wait_b(layer, 0)
        cross(0, 0)
        along0 = both_ways(0, 0)
        share(0, 0, 0)
        cross(1, 0)
        ready((1, 0, 0), (0, 0, 0))
        products(layer, lambda j: (j, chip(0, 0)), 2, out, every)
        pass_on(1, 0, along1)
        crossed[0, 0].wait_recv()
        along2 = both_ways(0, 1)
        share(0, 0, 1)
        pass_on(0, 0, along0)
        ready((1, 1, 0), (1, 3, 0))
        products(layer, lambda j: (1, chip(1 + 2 * j, 0)), 2, out, every)
        end_far(1, 0)
        end_cross(0)
        ready((0, 0, 1), (0, 1, 0), (0, 3, 0))
        products(layer, lambda j: (0, chip(3 + j, j % 2)), 3, out, every)
        pass_on(0, 1, along2)
        ready((1, 2, 0), (1, 0, 1))
        products(layer, lambda j: (1, chip(2 - 2 * j, j)), 2, out, every)
        end_cross(1)
        end_cross(3)
        ready((0, 1, 1), (0, 3, 1))
        products(layer, lambda j: (0, chip(1 + 2 * j, 1)), 2, out, every)
        end_far(0, 0)
        end_cross(2)
        ready((1, 1, 1), (1, 3, 1))
        products(layer, lambda j: (1, chip(1 + 2 * j, 1)), 2, out, every)
        end_far(0, 1)
        ready((0, 2, 0), (1, 2, 1), (0, 2, 1))
        for h in range(2):
            products(layer, lambda j: (j // 2, chip(2, (j + 1) // 2)), 3, out, rows_of[h])
            begin[h]()

    class ZFirst:
        def __init__(self, part, buf, made):
            self.part, self.buf, self.made = part, buf, made

        def start(self):
            up, down = (row, reps_dev(0, 1)), (row, reps_dev(0, 3))
            part, buf = self.part, self.buf
            self.raw = [
                remote(part((z + 2) % 4), buf.at[0], up),
                remote(part(4 + (z + 2) % 4), buf.at[1], down),
            ]
            self.second = [
                remote(part(4 + (z + 1) % 4), buf.at[3], up),
                remote(part((z + 3) % 4), buf.at[4], down),
            ]

        def pass_on(self):
            up, down = (row, reps_dev(0, 1)), (row, reps_dev(0, 3))
            buf, made = self.buf, self.made
            self.raw[0].wait_recv()
            made[0] = self.part((z + 1) % 4)[...] + buf[0]
            self.second.append(remote(made.at[0], buf.at[2], up))
            self.raw[1].wait_recv()
            made[1] = self.part(4 + (z + 3) % 4)[...] + buf[1]
            self.second.append(remote(made.at[1], buf.at[5], down))

        def cross(self):
            for copy in self.second:
                copy.wait_recv()
            other, buf = 1 - xl, self.buf
            self.made[2] = self.part(other * 4 + z)[...] + buf[2 + other] + buf[4 + other]
            self.last = remote(self.made.at[2], buf.at[6], (row, reps_dev(1, 0)))

        def total(self):
            buf = self.buf
            mine = self.part(rep)[...] + buf[2 + xl] + buf[4 + xl]
            self.last.wait_recv()
            return mine + buf[6]

    class XFirst:
        def __init__(self, part, buf, made):
            self.part, self.buf, self.made = part, buf, made
            self.n = made.shape[1] // 2

        def start(self):
            over = (row, reps_dev(1, 0))
            self.over = {
                b: remote(self.part(reps_dev(1, b)), self.buf.at[b], over) for b in (2, 1, 3, 0)
            }

        def near(self, b):
            self.over[b].wait_recv()
            return self.part(reps_dev(0, b))[...] + self.buf[b]

        def halves(self, ref):
            return ref.at[pl.ds(0, self.n)], ref.at[pl.ds(self.n, self.n)]

        def send_far(self):
            up, down = (row, reps_dev(0, 1)), (row, reps_dev(0, 3))
            made, buf = self.made, self.buf
            made[0] = self.near(2)
            (m0, m1), (b0, b1) = self.halves(made.at[0]), self.halves(buf.at[4])
            self.far = [remote(m0, b0, up), remote(m1, b1, down)]

        def send_near(self):
            up, down = (row, reps_dev(0, 1)), (row, reps_dev(0, 3))
            made, buf = self.made, self.buf
            made[1] = self.near(1)
            self.up, self.up_to = self.halves(made.at[1]), self.halves(buf.at[5])
            self.last = [remote(self.up[1], self.up_to[1], up)]
            made[2] = self.near(3)
            self.down, self.down_to = self.halves(made.at[2]), self.halves(buf.at[6])
            self.last.append(remote(self.down[0], self.down_to[0], down))

        def pass_on(self):
            up, down = (row, reps_dev(0, 1)), (row, reps_dev(0, 3))
            n, made, buf = self.n, self.made, self.buf
            self.far[0].wait_recv()
            made[1, 0:n] += buf[4, 0:n]
            self.last.append(remote(self.up[0], self.up_to[0], up))
            self.far[1].wait_recv()
            made[2, n:] += buf[4, n:]
            self.last.append(remote(self.down[1], self.down_to[1], down))

        def total(self):
            mine = self.near(0)
            for copy in self.last:
                copy.wait_recv()
            return mine + self.buf[5] + self.buf[6]

    def transform(total, layer):
        wh, wl = split(w_ref[layer])
        th, tl = split(total.reshape(128, 256))
        return jnp.maximum(mm(th, wh) + mm(th, wl) + mm(tl, wh), 0.0)

    def add_up(x_first, z_first, use):
        z_first.pass_on()
        x_first.send_far()
        z_first.cross()
        x_first.send_near()
        x_first.pass_on()
        use(1, z_first.total())
        use(0, x_first.total())

    for h in (1, 0):
        send_a(0, h, lambda p, h=h: x_ref.at[h, p, rep])
    hi[256] = jnp.zeros((128, 128), BF)
    lo[256] = jnp.zeros((128, 128), BF)

    def clear(i, carry):
        acc[i] = jnp.zeros((8, 8, 256), F32)
        acc_out[i] = jnp.zeros((8, 8, 256), F32)
        return carry

    lax.fori_loop(0, 32, clear, 0)
    convert(0, 6)
    turn(0, 1)
    turn(0, 0)
    convert(6, 256 // GROUP)

    def mid_part(h):
        return lambda k: acc.at[pl.ds(16 * h, 16), k]

    def end_part(h):
        return lambda k: acc_out.at[pl.ds(4 * k + 2 * h, 2)]

    mid = XFirst(mid_part(0), mx, mx_made), ZFirst(mid_part(1), mz, mz_made)
    end = XFirst(end_part(0), ex, ex_made), ZFirst(end_part(1), ez, ez_made)

    gather_and_multiply(
        0, acc, (range(8), range(8, 16)), (mid[0].start, mid[1].start)
    )

    def use_mid(h, total):
        hid[h] = transform(total, 0).reshape(16, 8, 256)
        send_a(1, h, lambda p: hid.at[h, p])

    add_up(*mid, use_mid)
    turn(1, 1)
    turn(1, 0)
    gather_and_multiply(
        1, acc_out, (range(0, 16, 2), range(1, 16, 2)), (end[0].start, end[1].start)
    )

    def use_end(h, total):
        o_ref[128 * h : 128 * h + 128] = transform(total, 1)

    add_up(*end, use_end)

    for copy in sent:
        copy.wait_send()
    for layer in range(2):
        for h in range(2):
            some = buf_a[layer][h].at[0:15]
            pltpu.make_async_copy(some, some, a_send.at[layer, h]).wait()
            some = send_b.at[layer, h, 0:7]
            pltpu.make_async_copy(some, some, b_send.at[layer, h]).wait()


def shards(features, adjacency_tiles, tile_rows, tile_cols, tile_counts, plan, weights):
    rows, cols, count = tile_rows[0, 0], tile_cols[0, 0], tile_counts[0, 0]
    slots = jnp.arange(256, dtype=jnp.int32)
    place = jnp.where(slots < count, rows * 32 + cols, -1)
    spots = jnp.arange(512, dtype=jnp.int32)
    pos = jnp.min(jnp.where(place[None, :] == spots[:, None], slots[None, :], 256), axis=1)
    piece = (16, 8, 256)
    flat = (2, 8, 8, 256)
    dma = pltpu.SemaphoreType.DMA
    return pl.pallas_call(
        kernel,
        name="graph_layers",
        out_shape=jax.ShapeDtypeStruct((256, 256), F32),
        in_specs=[
            pl.BlockSpec(memory_space=pltpu.SMEM),
            pl.BlockSpec(memory_space=pltpu.SMEM),
            pl.BlockSpec(memory_space=pl.ANY),
            pl.BlockSpec(memory_space=pl.ANY),
            pl.BlockSpec(memory_space=pltpu.VMEM),
        ],
        out_specs=pl.BlockSpec(memory_space=pltpu.VMEM),
        scratch_shapes=[
            pltpu.VMEM((STAGES, GROUP, 128, 128), F32),
            pltpu.VMEM((257, 128, 128), BF),
            pltpu.VMEM((257, 128, 128), BF),
            pltpu.VMEM((2, 2, 2, 16, 8, 8, 256), F32),
            pltpu.VMEM((32, 8, 8, 256), F32),
            pltpu.VMEM((32, 8, 8, 256), F32),
            pltpu.VMEM((16, 8, 256), F32),
            pltpu.VMEM((16, 8, 256), F32),
            pltpu.VMEM((16, 8, 256), F32),
            pltpu.VMEM((16, 8, 256), F32),
            pltpu.VMEM((2, 2, 8, 2, 8, 256), F32),
            pltpu.VMEM((2, 16, 8, 256), F32),
            pltpu.VMEM((256, 256), BF),
            pltpu.VMEM((256, 256), BF),
            pltpu.VMEM((7,) + piece, F32),
            pltpu.VMEM((3,) + piece, F32),
            pltpu.VMEM((7,) + piece, F32),
            pltpu.VMEM((3,) + piece, F32),
            pltpu.VMEM((7,) + flat, F32),
            pltpu.VMEM((3,) + flat, F32),
            pltpu.VMEM((7,) + flat, F32),
            pltpu.VMEM((3,) + flat, F32),
            dma((STAGES,)),
            dma((COPIES,)),
            dma((COPIES,)),
            dma((2, 2)),
            dma((2, 2)),
            dma((2, 2)),
            dma((2, 2)),
        ],
        compiler_params=pltpu.CompilerParams(
            collective_id=0, has_side_effects=True, vmem_limit_bytes=58 * 2**20
        ),
    )(
        pos,
        plan,
        features.reshape(2, 16, 8, 8, 256),
        adjacency_tiles.reshape(256, 128, 128),
        weights,
    )


def solution(mesh):
    return jax.shard_map(
        shards,
        mesh=mesh,
        in_specs=(
            P("row", None),
            P("row", "rep", None, None, None),
            P("row", "rep", None),
            P("row", "rep", None),
            P("row", "rep"),
            P(),
            P(),
        ),
        out_specs=P(("row", "rep"), None),
        check_vma=False,
    )
```

```python
import functools

import jax
import jax.numpy as jnp
from jax import lax
from jax.experimental import pallas as pl
from jax.experimental.pallas import tpu as pltpu
from jax.sharding import PartitionSpec as P

BF = jnp.bfloat16
F32 = jnp.float32
MESH = pl.DeviceIdType.MESH
Y, XH, C, XL, Z = 4, 2, 2, 2, 4
GROUP = 16
STAGES = 4
COPIES = 160


def mm(a, b):
    return jnp.dot(a, b, preferred_element_type=F32)


def split(v):
    high = v.astype(BF)
    return high, (v - high.astype(F32)).astype(BF)


def kernel(
    rows_ref, cols_ref, count_ref, plan_ref, x_ref, tiles, w_ref, o_ref,
    stage, hi, lo, land, acc, acc_out, big_0, big_1, send_b, hid, bh, bl, w_high, w_low,
    mx, mx_made, mz, mz_made, ex, ex_made, ez, ez_made,
    pos_made, pos, plan, pos_sem, plan_sem, stage_sem, ssem, rsem, a_send, a_recv, b_send, b_recv,
):
    row, rep = lax.axis_index("row"), lax.axis_index("rep")
    y, xh, c = row // 4, (row // 2) % 2, row % 2
    xl, z = rep // 4, rep % 4

    def rows_dev(dy, dx, dc):
        return ((y + dy) % 4) * 4 + ((xh + dx) % 2) * 2 + (c + dc) % 2

    def reps_dev(dx, dz):
        return ((xl + dx) % 2) * 4 + (z + dz) % 4

    plane = [(2, 1), (2, 0), (1, 1), (3, 1), (0, 1), (1, 0), (3, 0)]
    row_peers = [rows_dev(a, b, 0) for a, b in plane]
    near_peers = [(rows_dev(a, b, 0), reps_dev(b, 0)) for a, b in plane]
    rep_peers = [
        reps_dev(a, b) for a, b in ((1, 2), (0, 2), (1, 1), (1, 3), (1, 0), (0, 1), (0, 3))
    ]

    def load_tiles(g, slot):
        return pltpu.make_async_copy(
            tiles.at[pl.ds(g * GROUP, GROUP)], stage.at[slot], stage_sem.at[slot]
        )

    for g in range(STAGES):
        load_tiles(g, g).start()

    fetch_plan = pltpu.make_async_copy(plan_ref, plan, plan_sem)
    fetch_plan.start()
    barrier = pltpu.get_barrier_semaphore()
    for peer in row_peers + [rows_dev(0, 0, 1)]:
        pl.semaphore_signal(barrier, inc=1, device_id=(peer, rep), device_id_type=MESH)
    for peer in rep_peers:
        pl.semaphore_signal(barrier, inc=1, device_id=(row, peer), device_id_type=MESH)
    for (_, b), (peer, to) in zip(plane, near_peers):
        if b:
            pl.semaphore_signal(barrier, inc=1, device_id=(peer, to), device_id_type=MESH)
    pl.semaphore_wait(barrier, 19)

    used = [0]
    sent = []

    def remote(src, dst, dev):
        n = used[0]
        used[0] += 1
        copy = pltpu.make_async_remote_copy(
            src_ref=src, dst_ref=dst, send_sem=ssem.at[n], recv_sem=rsem.at[n],
            device_id=dev, device_id_type=MESH,
        )
        sent.append(copy)
        copy.start()
        return copy

    big = (big_0, big_1)
    here = row // 2

    def send_a(layer, source, peers):
        for peer, to in peers:
            pltpu.make_async_remote_copy(
                src_ref=source(peer // 2, to), dst_ref=big[layer].at[here, c],
                send_sem=a_send.at[layer], recv_sem=a_recv.at[layer],
                device_id=(peer, to), device_id_type=MESH,
            ).start()
        pltpu.make_async_copy(source(here, rep), big[layer].at[here, c], a_recv.at[layer]).start()

    def turn(layer):
        plane_part = big[layer].at[:, c]
        pltpu.make_async_copy(plane_part, plane_part, a_recv.at[layer]).wait()
        other = big[layer].at[:, c, :, 1 - c]
        remote(other, other, (rows_dev(0, 0, 1), rep)).wait_recv()
        for h in (1, 0):
            for k in range(8):
                for s in range(2):
                    r = plan[s, k]
                    send_b[layer, h, k, s] = big[layer][r // 2, r % 2, h, c]
            for peer in rep_peers:
                pltpu.make_async_remote_copy(
                    src_ref=send_b.at[layer, h, peer], dst_ref=land.at[layer, :, h, row, rep],
                    send_sem=b_send.at[layer, h], recv_sem=b_recv.at[layer, h],
                    device_id=(row, peer), device_id_type=MESH,
                ).start()
            pltpu.make_async_copy(
                send_b.at[layer, h, rep], land.at[layer, :, h, row, rep], b_recv.at[layer, h]
            ).start()

    def wait_b(layer, h):
        mine = land.at[layer, :, h, row]
        pltpu.make_async_copy(mine, mine, b_recv.at[layer, h]).wait()

    def place_tiles():
        slot = lax.broadcasted_iota(jnp.int32, (1, 256), 1)
        key = jnp.where(slot < count_ref[0, 0], rows_ref[...] * 32 + cols_ref[...], -1)
        down = lax.broadcasted_iota(jnp.int32, (128, 128), 0)
        spot = lax.broadcasted_iota(jnp.int32, (128, 128), 1)
        keys = [
            jnp.broadcast_to(key[:, 128 * n : 128 * n + 128], (128, 128)).T for n in range(2)
        ]
        for b in range(4):
            found = jnp.minimum(
                jnp.where(keys[0] == spot + 128 * b, down, 256),
                jnp.where(keys[1] == spot + 128 * b, down + 128, 256),
            )
            pos_made[b : b + 1] = jnp.min(found, axis=0, keepdims=True)
        pltpu.make_async_copy(pos_made, pos, pos_sem).start()

    def convert(first, last):
        def one(g, carry):
            slot = lax.rem(g, STAGES)
            load_tiles(g, slot).wait()

            def tile(t, inner):
                high, low = split(stage[slot, t])
                hi[g * GROUP + t] = high
                lo[g * GROUP + t] = low
                return inner

            lax.fori_loop(0, GROUP, tile, 0, unroll=4)

            @pl.when(g + STAGES < 256 // GROUP)
            def _():
                load_tiles(g + STAGES, slot).start()

            return carry

        lax.fori_loop(first, last, one, 0)

    def products(layer, tile_of, count, out, row_tiles):
        def one(j, carry):
            h, q = tile_of(j)
            t = h * 8 + q
            f0 = land[layer, 0, h, pl.ds(q * 2, 2)].reshape(128, 256)
            f1_ = land[layer, 1, h, pl.ds(q * 2, 2)].reshape(128, 256)
            bh[0:128], bl[0:128] = split(f0)
            bh[128:256], bl[128:256] = split(f1_)
            for i in row_tiles:
                a0, a1 = pos[i // 4, i % 4 * 32 + t], pos[i // 4, i % 4 * 32 + 16 + t]
                top = jnp.concatenate([hi[a0], hi[a1]], axis=1)
                low = jnp.concatenate([lo[a0], lo[a1]], axis=1)
                added = mm(top, bh[...]) + mm(top, bl[...]) + mm(low, bh[...])
                out[2 * i : 2 * i + 2] += added.reshape(2, 8, 8, 256)
            return carry

        lax.fori_loop(0, count, one, 0)

    def chip(dy, dx):
        return ((y + dy) % 4) * 2 + (xh + dx) % 2

    def gather_and_multiply(layer, out, rows_of, begin):
        every = range(16)
        core = {}

        def piece(h, dy, dx):
            return land.at[layer, :, h, chip(dy, dx) * 2 + c]

        def half(h, s, dy, dx):
            return land.at[layer, s, h, chip(dy, dx) * 2 + c]

        def move(ref, dy, dx, dc):
            return remote(ref, ref, (rows_dev(dy, dx, dc), rep))

        def share(h, dy, dx):
            core.setdefault((h, dy, dx), []).append(move(piece(h, dy, dx), 0, 0, 1))

        def ready(*keys):
            for key in keys:
                for copy in core[key]:
                    copy.wait_recv()

        def both_ways(h, dx):
            mine = piece(h, 0, dx)
            return move(mine, 1, 0, 0), move(mine, 3, 0, 0)

        far, crossed = {}, {}

        def cross(h, dy):
            crossed[h, dy] = move(piece(h, dy, 0), 0, 1, 0)

        def pass_on(h, dx, pair):
            pair[0].wait_recv()
            a = move(half(h, 0, 3, dx), 1, 0, 0)
            share(h, 3, dx)
            if h == 1:
                cross(h, 3)
            pair[1].wait_recv()
            b = move(half(h, 1, 1, dx), 3, 0, 0)
            share(h, 1, dx)
            if h == 1:
                cross(h, 1)
            far[h, dx] = (a, b)

        def end_far(h, dx):
            for copy in far[h, dx]:
                copy.wait_recv()
            share(h, 2, dx)
            if h == 1:
                cross(h, 2)

        def end_cross(dy):
            crossed[1, dy].wait_recv()
            share(1, dy, 1)

        wait_b(layer, 1)
        along1 = both_ways(1, 0)
        share(1, 0, 0)
        wait_b(layer, 0)
        cross(0, 0)
        along0 = both_ways(0, 0)
        share(0, 0, 0)
        cross(1, 0)
        ready((1, 0, 0), (0, 0, 0))
        products(layer, lambda j: (j, chip(0, 0)), 2, out, every)
        pass_on(1, 0, along1)
        crossed[0, 0].wait_recv()
        along2 = both_ways(0, 1)
        share(0, 0, 1)
        pass_on(0, 0, along0)
        ready((1, 1, 0), (1, 3, 0))
        products(layer, lambda j: (1, chip(1 + 2 * j, 0)), 2, out, every)
        end_far(1, 0)
        end_cross(0)
        ready((0, 0, 1), (0, 1, 0), (0, 3, 0))
        products(layer, lambda j: (0, chip(3 + j, j % 2)), 3, out, every)
        pass_on(0, 1, along2)
        ready((1, 2, 0), (1, 0, 1))
        products(layer, lambda j: (1, chip(2 - 2 * j, j)), 2, out, every)
        end_cross(1)
        end_cross(3)
        ready((0, 1, 1), (0, 3, 1))
        products(layer, lambda j: (0, chip(1 + 2 * j, 1)), 2, out, every)
        end_far(0, 0)
        end_cross(2)
        ready((1, 1, 1), (1, 3, 1))
        products(layer, lambda j: (1, chip(1 + 2 * j, 1)), 2, out, every)
        end_far(0, 1)
        ready((0, 2, 0), (1, 2, 1), (0, 2, 1))
        for h in range(2):
            products(layer, lambda j: (j // 2, chip(2, (j + 1) // 2)), 3, out, rows_of[h])
            begin[h]()

    class ZFirst:
        def __init__(self, part, buf, made):
            self.part, self.buf, self.made = part, buf, made

        def start(self):
            up, down = (row, reps_dev(0, 1)), (row, reps_dev(0, 3))
            part, buf = self.part, self.buf
            self.raw = [
                remote(part((z + 2) % 4), buf.at[0], up),
                remote(part(4 + (z + 2) % 4), buf.at[1], down),
            ]
            self.second = [
                remote(part(4 + (z + 1) % 4), buf.at[3], up),
                remote(part((z + 3) % 4), buf.at[4], down),
            ]

        def pass_on(self):
            up, down = (row, reps_dev(0, 1)), (row, reps_dev(0, 3))
            buf, made = self.buf, self.made
            self.raw[0].wait_recv()
            made[0] = self.part((z + 1) % 4)[...] + buf[0]
            self.second.append(remote(made.at[0], buf.at[2], up))
            self.raw[1].wait_recv()
            made[1] = self.part(4 + (z + 3) % 4)[...] + buf[1]
            self.second.append(remote(made.at[1], buf.at[5], down))

        def cross(self):
            for copy in self.second:
                copy.wait_recv()
            other, buf = 1 - xl, self.buf
            self.made[2] = self.part(other * 4 + z)[...] + buf[2 + other] + buf[4 + other]
            self.last = remote(self.made.at[2], buf.at[6], (row, reps_dev(1, 0)))

        def total(self):
            buf = self.buf
            mine = self.part(rep)[...] + buf[2 + xl] + buf[4 + xl]
            self.last.wait_recv()
            return mine + buf[6]

    class XFirst:
        def __init__(self, part, buf, made):
            self.part, self.buf, self.made = part, buf, made
            self.n = made.shape[1] // 2

        def start(self):
            over = (row, reps_dev(1, 0))
            self.over = {
                b: remote(self.part(reps_dev(1, b)), self.buf.at[b], over) for b in (2, 1, 3, 0)
            }

        def near(self, b):
            self.over[b].wait_recv()
            return self.part(reps_dev(0, b))[...] + self.buf[b]

        def halves(self, ref):
            return ref.at[pl.ds(0, self.n)], ref.at[pl.ds(self.n, self.n)]

        def send_far(self):
            up, down = (row, reps_dev(0, 1)), (row, reps_dev(0, 3))
            made, buf = self.made, self.buf
            made[0] = self.near(2)
            (m0, m1), (b0, b1) = self.halves(made.at[0]), self.halves(buf.at[4])
            self.far = [remote(m0, b0, up), remote(m1, b1, down)]

        def send_near(self):
            up, down = (row, reps_dev(0, 1)), (row, reps_dev(0, 3))
            made, buf = self.made, self.buf
            made[1] = self.near(1)
            self.up, self.up_to = self.halves(made.at[1]), self.halves(buf.at[5])
            self.last = [remote(self.up[1], self.up_to[1], up)]
            made[2] = self.near(3)
            self.down, self.down_to = self.halves(made.at[2]), self.halves(buf.at[6])
            self.last.append(remote(self.down[0], self.down_to[0], down))

        def pass_on(self):
            up, down = (row, reps_dev(0, 1)), (row, reps_dev(0, 3))
            n, made, buf = self.n, self.made, self.buf
            self.far[0].wait_recv()
            made[1, 0:n] += buf[4, 0:n]
            self.last.append(remote(self.up[0], self.up_to[0], up))
            self.far[1].wait_recv()
            made[2, n:] += buf[4, n:]
            self.last.append(remote(self.down[1], self.down_to[1], down))

        def total(self):
            mine = self.near(0)
            for copy in self.last:
                copy.wait_recv()
            return mine + self.buf[5] + self.buf[6]

    def transform(total, layer):
        wh, wl = w_high[layer], w_low[layer]
        th, tl = split(total.reshape(128, 256))
        return mm(th, wh) + mm(th, wl) + mm(tl, wh)

    def add_up(x_first, z_first, use):
        z_first.pass_on()
        x_first.send_far()
        z_first.cross()
        x_first.send_near()
        x_first.pass_on()
        use(1, z_first.total())
        use(0, x_first.total())

    send_a(0, lambda q, k: x_ref.at[:, pl.ds(2 * q, 2), k], near_peers)
    place_tiles()
    for layer in range(2):
        w_high[layer], w_low[layer] = split(w_ref[layer])
    hi[256] = jnp.zeros((128, 128), BF)
    lo[256] = jnp.zeros((128, 128), BF)

    def clear(i, carry):
        acc[i] = jnp.zeros((8, 8, 256), F32)
        acc_out[i] = jnp.zeros((8, 8, 256), F32)
        return carry

    lax.fori_loop(0, 32, clear, 0)
    convert(0, 4)
    fetch_plan.wait()
    turn(0)
    convert(4, 256 // GROUP)
    pltpu.make_async_copy(pos_made, pos, pos_sem).wait()

    def mid_part(h):
        return lambda k: acc.at[pl.ds(16 * h, 16), k]

    def end_part(h):
        return lambda k: acc_out.at[pl.ds(4 * k + 2 * h, 2)]

    mid = XFirst(mid_part(0), mx, mx_made), ZFirst(mid_part(1), mz, mz_made)
    end = XFirst(end_part(0), ex, ex_made), ZFirst(end_part(1), ez, ez_made)

    gather_and_multiply(
        0, acc, (range(8), range(8, 16)), (mid[0].start, mid[1].start)
    )

    def use_mid(h, total):
        hid[h] = jnp.maximum(transform(total, 0), 0.0).reshape(16, 8, 256)

    add_up(*mid, use_mid)
    send_a(1, lambda q, k: hid.at[:, pl.ds(2 * q, 2)], [(peer, rep) for peer in row_peers])
    turn(1)
    gather_and_multiply(
        1, acc_out, (range(0, 16, 2), range(1, 16, 2)), (end[0].start, end[1].start)
    )

    def use_end(h, total):
        o_ref[128 * h : 128 * h + 128] = transform(total, 1)

    add_up(*end, use_end)

    for copy in sent:
        copy.wait_send()
    for layer in range(2):
        some = big[layer].at[0:7, 0]
        pltpu.make_async_copy(some, some, a_send.at[layer]).wait()
        for h in range(2):
            some = send_b.at[layer, h, 0:7]
            pltpu.make_async_copy(some, some, b_send.at[layer, h]).wait()


def shards(features, adjacency_tiles, tile_rows, tile_cols, tile_counts, plan, weights):
    piece = (16, 8, 256)
    flat = (2, 8, 8, 256)
    dma = pltpu.SemaphoreType.DMA
    product = pl.pallas_call(
        kernel,
        name="graph_layers",
        out_shape=jax.ShapeDtypeStruct((256, 256), F32),
        in_specs=[
            pl.BlockSpec(memory_space=pltpu.VMEM),
            pl.BlockSpec(memory_space=pltpu.VMEM),
            pl.BlockSpec(memory_space=pltpu.SMEM),
            pl.BlockSpec(memory_space=pl.ANY),
            pl.BlockSpec(memory_space=pl.ANY),
            pl.BlockSpec(memory_space=pl.ANY),
            pl.BlockSpec(memory_space=pltpu.VMEM),
        ],
        out_specs=pl.BlockSpec(memory_space=pltpu.VMEM),
        scratch_shapes=[
            pltpu.VMEM((STAGES, GROUP, 128, 128), F32),
            pltpu.VMEM((257, 128, 128), BF),
            pltpu.VMEM((257, 128, 128), BF),
            pltpu.VMEM((2, 2, 2, 16, 8, 8, 256), F32),
            pltpu.VMEM((32, 8, 8, 256), F32),
            pltpu.VMEM((32, 8, 8, 256), F32),
            pltpu.VMEM((8, 2, 2, 2, 8, 256), F32),
            pltpu.VMEM((8, 2, 2, 2, 8, 256), F32),
            pltpu.VMEM((2, 2, 8, 2, 8, 256), F32),
            pltpu.VMEM((2, 16, 8, 256), F32),
            pltpu.VMEM((256, 256), BF),
            pltpu.VMEM((256, 256), BF),
            pltpu.VMEM((2, 256, 256), BF),
            pltpu.VMEM((2, 256, 256), BF),
            pltpu.VMEM((7,) + piece, F32),
            pltpu.VMEM((3,) + piece, F32),
            pltpu.VMEM((7,) + piece, F32),
            pltpu.VMEM((3,) + piece, F32),
            pltpu.VMEM((7,) + flat, F32),
            pltpu.VMEM((3,) + flat, F32),
            pltpu.VMEM((7,) + flat, F32),
            pltpu.VMEM((3,) + flat, F32),
            pltpu.VMEM((4, 128), jnp.int32),
            pltpu.SMEM((4, 128), jnp.int32),
            pltpu.SMEM((2, 8), jnp.int32),
            dma,
            dma,
            dma((STAGES,)),
            dma((COPIES,)),
            dma((COPIES,)),
            dma((2,)),
            dma((2,)),
            dma((2, 2)),
            dma((2, 2)),
        ],
        compiler_params=pltpu.CompilerParams(
            collective_id=0, has_side_effects=True, vmem_limit_bytes=58 * 2**20
        ),
    )(
        tile_rows.reshape(1, 256),
        tile_cols.reshape(1, 256),
        tile_counts,
        plan.T,
        features.reshape(2, 16, 8, 8, 256),
        adjacency_tiles.reshape(256, 128, 128),
        weights,
    )
    return jnp.maximum(product, 0.0)


def solution(mesh):
    return jax.shard_map(
        shards,
        mesh=mesh,
        in_specs=(
            P("row", None),
            P("row", "rep", None, None, None),
            P("row", "rep", None),
            P("row", "rep", None),
            P("row", "rep"),
            P(),
            P(),
        ),
        out_specs=P(("row", "rep"), None),
        check_vma=False,
    )
```

```python
import functools

import jax
import jax.numpy as jnp
from jax import lax
from jax.experimental import pallas as pl
from jax.experimental.pallas import tpu as pltpu
from jax.sharding import PartitionSpec as P

BF = jnp.bfloat16
F32 = jnp.float32
MESH = pl.DeviceIdType.MESH
Y, XH, C, XL, Z = 4, 2, 2, 2, 4
GROUP = 16
STAGES = 4
COPIES = 160


def mm(a, b):
    return jnp.dot(a, b, preferred_element_type=F32)


def split(v):
    high = v.astype(BF)
    return high, (v - high.astype(F32)).astype(BF)


def kernel(
    rows_ref, cols_ref, count_ref, plan_ref, x_ref, tiles, w_ref, o_ref,
    stage, hi, lo, land, acc, acc_out, big_0, big_10, big_11, send_b, hid, bh, bl, w_high, w_low,
    mx, mx_made, mz, mz_made, ex, ex_made, ez, ez_made,
    pos_made, pos, plan, pos_sem, plan_sem, stage_sem, ssem, rsem, a_send, a_recv, b_send, b_recv,
):
    row, rep = lax.axis_index("row"), lax.axis_index("rep")
    y, xh, c = row // 4, (row // 2) % 2, row % 2
    xl, z = rep // 4, rep % 4

    def rows_dev(dy, dx, dc):
        return ((y + dy) % 4) * 4 + ((xh + dx) % 2) * 2 + (c + dc) % 2

    def reps_dev(dx, dz):
        return ((xl + dx) % 2) * 4 + (z + dz) % 4

    plane = [(2, 1), (2, 0), (1, 1), (3, 1), (0, 1), (1, 0), (3, 0)]
    row_peers = [rows_dev(a, b, 0) for a, b in plane]
    near_peers = [(rows_dev(a, b, 0), reps_dev(b, 0)) for a, b in plane]
    rep_peers = [
        reps_dev(a, b) for a, b in ((1, 2), (0, 2), (1, 1), (1, 3), (1, 0), (0, 1), (0, 3))
    ]

    def load_tiles(g, slot):
        return pltpu.make_async_copy(
            tiles.at[pl.ds(g * GROUP, GROUP)], stage.at[slot], stage_sem.at[slot]
        )

    for g in range(STAGES):
        load_tiles(g, g).start()

    fetch_plan = pltpu.make_async_copy(plan_ref, plan, plan_sem)
    fetch_plan.start()
    barrier = pltpu.get_barrier_semaphore()
    for peer in row_peers + [rows_dev(0, 0, 1)]:
        pl.semaphore_signal(barrier, inc=1, device_id=(peer, rep), device_id_type=MESH)
    for peer in rep_peers:
        pl.semaphore_signal(barrier, inc=1, device_id=(row, peer), device_id_type=MESH)
    for (_, b), (peer, to) in zip(plane, near_peers):
        if b:
            pl.semaphore_signal(barrier, inc=1, device_id=(peer, to), device_id_type=MESH)
    pl.semaphore_wait(barrier, 19)

    used = [0]
    sent = []

    def remote(src, dst, dev):
        n = used[0]
        used[0] += 1
        copy = pltpu.make_async_remote_copy(
            src_ref=src, dst_ref=dst, send_sem=ssem.at[n], recv_sem=rsem.at[n],
            device_id=dev, device_id_type=MESH,
        )
        sent.append(copy)
        copy.start()
        return copy

    big = (big_0, big_10, big_11)
    here = row // 2

    def send_a(n, source, peers):
        for peer, to in peers:
            pltpu.make_async_remote_copy(
                src_ref=source(peer // 2, to), dst_ref=big[n].at[here, c],
                send_sem=a_send.at[n], recv_sem=a_recv.at[n],
                device_id=(peer, to), device_id_type=MESH,
            ).start()
        pltpu.make_async_copy(source(here, rep), big[n].at[here, c], a_recv.at[n]).start()

    def turn(layer, n, chunks):
        plane_part = big[n].at[:, c]
        pltpu.make_async_copy(plane_part, plane_part, a_recv.at[n]).wait()
        other = big[n].at[:, c, :, 1 - c]
        remote(other, other, (rows_dev(0, 0, 1), rep)).wait_recv()
        for at, h in chunks:
            for k in range(8):
                for s in range(2):
                    r = plan[s, k]
                    send_b[layer, h, k, s] = big[n][r // 2, r % 2, at, c]
            for peer in rep_peers:
                pltpu.make_async_remote_copy(
                    src_ref=send_b.at[layer, h, peer], dst_ref=land.at[layer, :, h, row, rep],
                    send_sem=b_send.at[layer, h], recv_sem=b_recv.at[layer, h],
                    device_id=(row, peer), device_id_type=MESH,
                ).start()
            pltpu.make_async_copy(
                send_b.at[layer, h, rep], land.at[layer, :, h, row, rep], b_recv.at[layer, h]
            ).start()

    def wait_b(layer, h):
        mine = land.at[layer, :, h, row]
        pltpu.make_async_copy(mine, mine, b_recv.at[layer, h]).wait()

    def place_tiles():
        slot = lax.broadcasted_iota(jnp.int32, (1, 256), 1)
        key = jnp.where(slot < count_ref[0, 0], rows_ref[...] * 32 + cols_ref[...], -1)
        down = lax.broadcasted_iota(jnp.int32, (128, 128), 0)
        spot = lax.broadcasted_iota(jnp.int32, (128, 128), 1)
        keys = [
            jnp.broadcast_to(key[:, 128 * n : 128 * n + 128], (128, 128)).T for n in range(2)
        ]
        for b in range(4):
            found = jnp.minimum(
                jnp.where(keys[0] == spot + 128 * b, down, 256),
                jnp.where(keys[1] == spot + 128 * b, down + 128, 256),
            )
            pos_made[b : b + 1] = jnp.min(found, axis=0, keepdims=True)
        pltpu.make_async_copy(pos_made, pos, pos_sem).start()

    def convert(first, last):
        def one(g, carry):
            slot = lax.rem(g, STAGES)
            load_tiles(g, slot).wait()

            def tile(t, inner):
                high, low = split(stage[slot, t])
                hi[g * GROUP + t] = high
                lo[g * GROUP + t] = low
                return inner

            lax.fori_loop(0, GROUP, tile, 0, unroll=4)

            @pl.when(g + STAGES < 256 // GROUP)
            def _():
                load_tiles(g + STAGES, slot).start()

            return carry

        lax.fori_loop(first, last, one, 0)

    def products(layer, chips, out, row_tiles, fresh=True):
        right = []
        for n, (h, q) in enumerate(chips):
            if fresh:
                for s in range(2):
                    part = land[layer, s, h, pl.ds(q * 2, 2)].reshape(128, 256)
                    r = slice(128 * s, 128 * s + 128)
                    bh[n, r], bl[n, r] = split(part)
            right += [bh[n], bh[n], bl[n]]
        right = jnp.concatenate(right, axis=0)
        for i in row_tiles:
            left = []
            for h, q in chips:
                t = h * 8 + q
                a0, a1 = pos[i // 4, i % 4 * 32 + t], pos[i // 4, i % 4 * 32 + 16 + t]
                top0, top1 = hi[a0], hi[a1]
                left += [top0, top1, lo[a0], lo[a1], top0, top1]
            added = mm(jnp.concatenate(left, axis=1), right)
            out[2 * i : 2 * i + 2] += added.reshape(2, 8, 8, 256)

    def chip(dy, dx):
        return ((y + dy) % 4) * 2 + (xh + dx) % 2

    def gather_and_multiply(layer, out, rows_of, begin):
        every = range(16)
        core = {}

        def piece(h, dy, dx):
            return land.at[layer, :, h, chip(dy, dx) * 2 + c]

        def half(h, s, dy, dx):
            return land.at[layer, s, h, chip(dy, dx) * 2 + c]

        def move(ref, dy, dx, dc):
            return remote(ref, ref, (rows_dev(dy, dx, dc), rep))

        def share(h, dy, dx):
            core.setdefault((h, dy, dx), []).append(move(piece(h, dy, dx), 0, 0, 1))

        def ready(*keys):
            for key in keys:
                for copy in core[key]:
                    copy.wait_recv()

        def both_ways(h, dx):
            mine = piece(h, 0, dx)
            return move(mine, 1, 0, 0), move(mine, 3, 0, 0)

        far, crossed = {}, {}

        def cross(h, dy):
            crossed[h, dy] = move(piece(h, dy, 0), 0, 1, 0)

        def pass_on(h, dx, pair):
            pair[0].wait_recv()
            a = move(half(h, 0, 3, dx), 1, 0, 0)
            share(h, 3, dx)
            if h == 1:
                cross(h, 3)
            pair[1].wait_recv()
            b = move(half(h, 1, 1, dx), 3, 0, 0)
            share(h, 1, dx)
            if h == 1:
                cross(h, 1)
            far[h, dx] = (a, b)

        def end_far(h, dx):
            for copy in far[h, dx]:
                copy.wait_recv()
            share(h, 2, dx)
            if h == 1:
                cross(h, 2)

        def end_cross(dy):
            crossed[1, dy].wait_recv()
            share(1, dy, 1)

        wait_b(layer, 1)
        along1 = both_ways(1, 0)
        share(1, 0, 0)
        wait_b(layer, 0)
        cross(0, 0)
        along0 = both_ways(0, 0)
        share(0, 0, 0)
        cross(1, 0)
        ready((1, 0, 0), (0, 0, 0))
        products(layer, [(0, chip(0, 0)), (1, chip(0, 0))], out, every)
        pass_on(1, 0, along1)
        crossed[0, 0].wait_recv()
        along2 = both_ways(0, 1)
        share(0, 0, 1)
        pass_on(0, 0, along0)
        ready((1, 1, 0), (1, 3, 0))
        products(layer, [(1, chip(1, 0)), (1, chip(3, 0))], out, every)
        end_far(1, 0)
        end_cross(0)
        ready((0, 0, 1), (0, 3, 0))
        products(layer, [(0, chip(3, 0)), (0, chip(0, 1))], out, every)
        pass_on(0, 1, along2)
        ready((0, 1, 0), (1, 2, 0), (1, 0, 1))
        products(layer, [(0, chip(1, 0)), (1, chip(2, 0)), (1, chip(0, 1))], out, every)
        end_cross(1)
        end_cross(3)
        end_far(0, 0)
        ready((0, 1, 1), (0, 3, 1))
        products(layer, [(0, chip(1, 1)), (0, chip(3, 1))], out, every)
        end_cross(2)
        ready((1, 1, 1), (1, 3, 1), (0, 2, 0))
        products(layer, [(1, chip(1, 1)), (1, chip(3, 1)), (0, chip(2, 0))], out, every)
        end_far(0, 1)
        ready((1, 2, 1), (0, 2, 1))
        for h in range(2):
            products(
                layer, [(0, chip(2, 1)), (1, chip(2, 1))], out, rows_of[h], h == 0
            )
            begin[h]()

    class ZFirst:
        def __init__(self, part, buf, made):
            self.part, self.buf, self.made = part, buf, made

        def start(self):
            up, down = (row, reps_dev(0, 1)), (row, reps_dev(0, 3))
            part, buf = self.part, self.buf
            self.raw = [
                remote(part((z + 2) % 4), buf.at[0], up),
                remote(part(4 + (z + 2) % 4), buf.at[1], down),
            ]
            self.second = [
                remote(part(4 + (z + 1) % 4), buf.at[3], up),
                remote(part((z + 3) % 4), buf.at[4], down),
            ]

        def pass_on(self):
            up, down = (row, reps_dev(0, 1)), (row, reps_dev(0, 3))
            buf, made = self.buf, self.made
            self.raw[0].wait_recv()
            made[0] = self.part((z + 1) % 4)[...] + buf[0]
            self.second.append(remote(made.at[0], buf.at[2], up))
            self.raw[1].wait_recv()
            made[1] = self.part(4 + (z + 3) % 4)[...] + buf[1]
            self.second.append(remote(made.at[1], buf.at[5], down))

        def cross(self):
            for copy in self.second:
                copy.wait_recv()
            other, buf = 1 - xl, self.buf
            self.made[2] = self.part(other * 4 + z)[...] + buf[2 + other] + buf[4 + other]
            self.last = remote(self.made.at[2], buf.at[6], (row, reps_dev(1, 0)))

        def total(self):
            buf = self.buf
            mine = self.part(rep)[...] + buf[2 + xl] + buf[4 + xl]
            self.last.wait_recv()
            return mine + buf[6]

    class XFirst:
        def __init__(self, part, buf, made):
            self.part, self.buf, self.made = part, buf, made
            self.n = made.shape[1] // 2

        def start(self):
            over = (row, reps_dev(1, 0))
            self.over = {
                b: remote(self.part(reps_dev(1, b)), self.buf.at[b], over) for b in (2, 1, 3, 0)
            }

        def near(self, b):
            self.over[b].wait_recv()
            return self.part(reps_dev(0, b))[...] + self.buf[b]

        def halves(self, ref):
            return ref.at[pl.ds(0, self.n)], ref.at[pl.ds(self.n, self.n)]

        def send_far(self):
            up, down = (row, reps_dev(0, 1)), (row, reps_dev(0, 3))
            made, buf = self.made, self.buf
            made[0] = self.near(2)
            (m0, m1), (b0, b1) = self.halves(made.at[0]), self.halves(buf.at[4])
            self.far = [remote(m0, b0, up), remote(m1, b1, down)]

        def send_near(self):
            up, down = (row, reps_dev(0, 1)), (row, reps_dev(0, 3))
            made, buf = self.made, self.buf
            made[1] = self.near(1)
            self.up, self.up_to = self.halves(made.at[1]), self.halves(buf.at[5])
            self.last = [remote(self.up[1], self.up_to[1], up)]
            made[2] = self.near(3)
            self.down, self.down_to = self.halves(made.at[2]), self.halves(buf.at[6])
            self.last.append(remote(self.down[0], self.down_to[0], down))

        def pass_on(self):
            up, down = (row, reps_dev(0, 1)), (row, reps_dev(0, 3))
            n, made, buf = self.n, self.made, self.buf
            self.far[0].wait_recv()
            made[1, 0:n] += buf[4, 0:n]
            self.last.append(remote(self.up[0], self.up_to[0], up))
            self.far[1].wait_recv()
            made[2, n:] += buf[4, n:]
            self.last.append(remote(self.down[1], self.down_to[1], down))

        def total(self):
            mine = self.near(0)
            for copy in self.last:
                copy.wait_recv()
            return mine + self.buf[5] + self.buf[6]

    def transform(total, layer):
        wh, wl = w_high[layer], w_low[layer]
        th, tl = split(total.reshape(128, 256))
        return mm(th, wh) + mm(th, wl) + mm(tl, wh)

    def add_up(x_first, z_first, use):
        z_first.pass_on()
        x_first.send_far()
        z_first.cross()
        x_first.send_near()
        x_first.pass_on()
        use(1, z_first.total())
        use(0, x_first.total())

    send_a(0, lambda q, k: x_ref.at[:, pl.ds(2 * q, 2), k], near_peers)
    place_tiles()
    for layer in range(2):
        w_high[layer], w_low[layer] = split(w_ref[layer])
    hi[256] = jnp.zeros((128, 128), BF)
    lo[256] = jnp.zeros((128, 128), BF)

    def clear(i, carry):
        acc[i] = jnp.zeros((8, 8, 256), F32)
        acc_out[i] = jnp.zeros((8, 8, 256), F32)
        return carry

    lax.fori_loop(0, 32, clear, 0)
    convert(0, 4)
    fetch_plan.wait()
    turn(0, 0, ((1, 1), (0, 0)))
    convert(4, 256 // GROUP)
    pltpu.make_async_copy(pos_made, pos, pos_sem).wait()

    def mid_part(h):
        return lambda k: acc.at[pl.ds(16 * h, 16), k]

    def end_part(h):
        return lambda k: acc_out.at[pl.ds(4 * k + 2 * h, 2)]

    mid = XFirst(mid_part(0), mx, mx_made), ZFirst(mid_part(1), mz, mz_made)
    end = XFirst(end_part(0), ex, ex_made), ZFirst(end_part(1), ez, ez_made)

    gather_and_multiply(
        0, acc, (range(8), range(8, 16)), (mid[0].start, mid[1].start)
    )

    def use_mid(h, total):
        hid[h] = jnp.maximum(transform(total, 0), 0.0).reshape(16, 8, 256)
        send_a(
            1 + h,
            lambda q, k: hid.at[pl.ds(h, 1), pl.ds(2 * q, 2)],
            [(peer, rep) for peer in row_peers],
        )

    add_up(*mid, use_mid)
    turn(1, 2, ((0, 1),))
    turn(1, 1, ((0, 0),))
    gather_and_multiply(
        1, acc_out, (range(0, 16, 2), range(1, 16, 2)), (end[0].start, end[1].start)
    )

    def use_end(h, total):
        o_ref[128 * h : 128 * h + 128] = transform(total, 1)

    add_up(*end, use_end)

    for copy in sent:
        copy.wait_send()
    for n in range(3):
        some = big[n].at[0:7, 0]
        pltpu.make_async_copy(some, some, a_send.at[n]).wait()
    for layer in range(2):
        for h in range(2):
            some = send_b.at[layer, h, 0:7]
            pltpu.make_async_copy(some, some, b_send.at[layer, h]).wait()


def shards(features, adjacency_tiles, tile_rows, tile_cols, tile_counts, plan, weights):
    piece = (16, 8, 256)
    flat = (2, 8, 8, 256)
    dma = pltpu.SemaphoreType.DMA
    product = pl.pallas_call(
        kernel,
        name="graph_layers",
        out_shape=jax.ShapeDtypeStruct((256, 256), F32),
        in_specs=[
            pl.BlockSpec(memory_space=pltpu.VMEM),
            pl.BlockSpec(memory_space=pltpu.VMEM),
            pl.BlockSpec(memory_space=pltpu.SMEM),
            pl.BlockSpec(memory_space=pl.ANY),
            pl.BlockSpec(memory_space=pl.ANY),
            pl.BlockSpec(memory_space=pl.ANY),
            pl.BlockSpec(memory_space=pltpu.VMEM),
        ],
        out_specs=pl.BlockSpec(memory_space=pltpu.VMEM),
        scratch_shapes=[
            pltpu.VMEM((STAGES, GROUP, 128, 128), F32),
            pltpu.VMEM((257, 128, 128), BF),
            pltpu.VMEM((257, 128, 128), BF),
            pltpu.VMEM((2, 2, 2, 16, 8, 8, 256), F32),
            pltpu.VMEM((32, 8, 8, 256), F32),
            pltpu.VMEM((32, 8, 8, 256), F32),
            pltpu.VMEM((8, 2, 2, 2, 8, 256), F32),
            pltpu.VMEM((8, 2, 1, 2, 8, 256), F32),
            pltpu.VMEM((8, 2, 1, 2, 8, 256), F32),
            pltpu.VMEM((2, 2, 8, 2, 8, 256), F32),
            pltpu.VMEM((2, 16, 8, 256), F32),
            pltpu.VMEM((3, 256, 256), BF),
            pltpu.VMEM((3, 256, 256), BF),
            pltpu.VMEM((2, 256, 256), BF),
            pltpu.VMEM((2, 256, 256), BF),
            pltpu.VMEM((7,) + piece, F32),
            pltpu.VMEM((3,) + piece, F32),
            pltpu.VMEM((7,) + piece, F32),
            pltpu.VMEM((3,) + piece, F32),
            pltpu.VMEM((7,) + flat, F32),
            pltpu.VMEM((3,) + flat, F32),
            pltpu.VMEM((7,) + flat, F32),
            pltpu.VMEM((3,) + flat, F32),
            pltpu.VMEM((4, 128), jnp.int32),
            pltpu.SMEM((4, 128), jnp.int32),
            pltpu.SMEM((2, 8), jnp.int32),
            dma,
            dma,
            dma((STAGES,)),
            dma((COPIES,)),
            dma((COPIES,)),
            dma((3,)),
            dma((3,)),
            dma((2, 2)),
            dma((2, 2)),
        ],
        compiler_params=pltpu.CompilerParams(
            collective_id=0, has_side_effects=True, vmem_limit_bytes=58 * 2**20
        ),
    )(
        tile_rows.reshape(1, 256),
        tile_cols.reshape(1, 256),
        tile_counts,
        plan.T,
        features.reshape(2, 16, 8, 8, 256),
        adjacency_tiles.reshape(256, 128, 128),
        weights,
    )
    return jnp.maximum(product, 0.0)


def solution(mesh):
    return jax.shard_map(
        shards,
        mesh=mesh,
        in_specs=(
            P("row", None),
            P("row", "rep", None, None, None),
            P("row", "rep", None),
            P("row", "rep", None),
            P("row", "rep"),
            P(),
            P(),
        ),
        out_specs=P(("row", "rep"), None),
        check_vma=False,
    )
```

```python
import functools

import jax
import jax.numpy as jnp
from jax import lax
from jax.experimental import pallas as pl
from jax.experimental.pallas import tpu as pltpu
from jax.sharding import PartitionSpec as P

BF = jnp.bfloat16
F32 = jnp.float32
MESH = pl.DeviceIdType.MESH
Y, XH, C, XL, Z = 4, 2, 2, 2, 4
GROUP = 16
STAGES = 4
COPIES = 160


def mm(a, b):
    return jnp.dot(a, b, preferred_element_type=F32)


def split(v):
    high = v.astype(BF)
    return high, (v - high.astype(F32)).astype(BF)


def kernel(
    rows_ref, cols_ref, count_ref, plan_ref, x_ref, tiles, w_ref, o_ref,
    stage, hi, lo, land, acc, acc_out, big_0, big_10, big_11, send_b, hid, bh, bl, w_high, w_low,
    mx, mx_made, mz, mz_made, ex, ex_made, ez, ez_made,
    pos_made, pos, plan, pos_sem, plan_sem, stage_sem, ssem, rsem, a_send, a_recv, b_send, b_recv,
):
    row, rep = lax.axis_index("row"), lax.axis_index("rep")
    y, xh, c = row // 4, (row // 2) % 2, row % 2
    xl, z = rep // 4, rep % 4

    def rows_dev(dy, dx, dc):
        return ((y + dy) % 4) * 4 + ((xh + dx) % 2) * 2 + (c + dc) % 2

    def reps_dev(dx, dz):
        return ((xl + dx) % 2) * 4 + (z + dz) % 4

    plane = [(2, 1), (2, 0), (1, 1), (3, 1), (0, 1), (1, 0), (3, 0)]
    row_peers = [rows_dev(a, b, 0) for a, b in plane]
    near_peers = [(rows_dev(a, b, 0), reps_dev(b, 0)) for a, b in plane]
    rep_peers = [
        reps_dev(a, b) for a, b in ((1, 2), (0, 2), (1, 1), (1, 3), (1, 0), (0, 1), (0, 3))
    ]

    def load_tiles(g, slot):
        return pltpu.make_async_copy(
            tiles.at[pl.ds(g * GROUP, GROUP)], stage.at[slot], stage_sem.at[slot]
        )

    for g in range(STAGES):
        load_tiles(g, g).start()

    fetch_plan = pltpu.make_async_copy(plan_ref, plan, plan_sem)
    fetch_plan.start()
    barrier = pltpu.get_barrier_semaphore()
    for peer in row_peers + [rows_dev(0, 0, 1)]:
        pl.semaphore_signal(barrier, inc=1, device_id=(peer, rep), device_id_type=MESH)
    for peer in rep_peers:
        pl.semaphore_signal(barrier, inc=1, device_id=(row, peer), device_id_type=MESH)
    for (_, b), (peer, to) in zip(plane, near_peers):
        if b:
            pl.semaphore_signal(barrier, inc=1, device_id=(peer, to), device_id_type=MESH)
    pl.semaphore_wait(barrier, 19)

    used = [0]
    sent = []

    def remote(src, dst, dev):
        n = used[0]
        used[0] += 1
        copy = pltpu.make_async_remote_copy(
            src_ref=src, dst_ref=dst, send_sem=ssem.at[n], recv_sem=rsem.at[n],
            device_id=dev, device_id_type=MESH,
        )
        sent.append(copy)
        copy.start()
        return copy

    big = (big_0, big_10, big_11)
    here = row // 2

    def send_a(n, source, peers):
        for peer, to in peers:
            pltpu.make_async_remote_copy(
                src_ref=source(peer // 2, to), dst_ref=big[n].at[here, c],
                send_sem=a_send.at[n], recv_sem=a_recv.at[n],
                device_id=(peer, to), device_id_type=MESH,
            ).start()
        pltpu.make_async_copy(source(here, rep), big[n].at[here, c], a_recv.at[n]).start()

    def turn(layer, n, chunks):
        plane_part = big[n].at[:, c]
        pltpu.make_async_copy(plane_part, plane_part, a_recv.at[n]).wait()
        other = big[n].at[:, c, :, 1 - c]
        remote(other, other, (rows_dev(0, 0, 1), rep)).wait_recv()
        for at, h in chunks:
            for k in range(8):
                for s in range(2):
                    r = plan[s, k]
                    send_b[layer, h, k, s] = big[n][r // 2, r % 2, at, c]
            for peer in rep_peers:
                pltpu.make_async_remote_copy(
                    src_ref=send_b.at[layer, h, peer], dst_ref=land.at[layer, :, h, row, rep],
                    send_sem=b_send.at[layer, h], recv_sem=b_recv.at[layer, h],
                    device_id=(row, peer), device_id_type=MESH,
                ).start()
            pltpu.make_async_copy(
                send_b.at[layer, h, rep], land.at[layer, :, h, row, rep], b_recv.at[layer, h]
            ).start()

    def wait_b(layer, h):
        mine = land.at[layer, :, h, row]
        pltpu.make_async_copy(mine, mine, b_recv.at[layer, h]).wait()

    def place_tiles():
        slot = lax.broadcasted_iota(jnp.int32, (1, 256), 1)
        key = jnp.where(slot < count_ref[0, 0], rows_ref[...] * 32 + cols_ref[...], -1)
        down = lax.broadcasted_iota(jnp.int32, (128, 128), 0)
        spot = lax.broadcasted_iota(jnp.int32, (128, 128), 1)
        keys = [
            jnp.broadcast_to(key[:, 128 * n : 128 * n + 128], (128, 128)).T for n in range(2)
        ]
        for b in range(4):
            found = jnp.minimum(
                jnp.where(keys[0] == spot + 128 * b, down, 256),
                jnp.where(keys[1] == spot + 128 * b, down + 128, 256),
            )
            pos_made[b : b + 1] = jnp.min(found, axis=0, keepdims=True)
        pltpu.make_async_copy(pos_made, pos, pos_sem).start()

    def convert(first, last):
        def one(g, carry):
            slot = lax.rem(g, STAGES)
            load_tiles(g, slot).wait()

            def tile(t, inner):
                high, low = split(stage[slot, t])
                hi[g * GROUP + t] = high
                lo[g * GROUP + t] = low
                return inner

            lax.fori_loop(0, GROUP, tile, 0, unroll=4)

            @pl.when(g + STAGES < 256 // GROUP)
            def _():
                load_tiles(g + STAGES, slot).start()

            return carry

        lax.fori_loop(first, last, one, 0)

    def products(layer, chips, out, row_tiles, fresh=True):
        right = []
        for n, (h, q) in enumerate(chips):
            if fresh:
                for s in range(2):
                    part = land[layer, s, h, pl.ds(q * 2, 2)].reshape(128, 256)
                    r = slice(128 * s, 128 * s + 128)
                    bh[n, r], bl[n, r] = split(part)
            right += [bh[n], bh[n], bl[n]]
        right = jnp.concatenate(right, axis=0)
        for i in row_tiles:
            left = []
            for h, q in chips:
                t = h * 8 + q
                a0, a1 = pos[i // 4, i % 4 * 32 + t], pos[i // 4, i % 4 * 32 + 16 + t]
                top0, top1 = hi[a0], hi[a1]
                left += [top0, top1, lo[a0], lo[a1], top0, top1]
            added = mm(jnp.concatenate(left, axis=1), right)
            out[2 * i : 2 * i + 2] += added.reshape(2, 8, 8, 256)

    def chip(dy, dx):
        return ((y + dy) % 4) * 2 + (xh + dx) % 2

    def gather_and_multiply(layer, out, rows_of, begin):
        every = range(16)
        core = {}

        def piece(h, dy, dx):
            return land.at[layer, :, h, chip(dy, dx) * 2 + c]

        def half(h, s, dy, dx):
            return land.at[layer, s, h, chip(dy, dx) * 2 + c]

        def move(ref, dy, dx, dc):
            return remote(ref, ref, (rows_dev(dy, dx, dc), rep))

        def share(h, dy, dx):
            core.setdefault((h, dy, dx), []).append(move(piece(h, dy, dx), 0, 0, 1))

        def ready(*keys):
            for key in keys:
                for copy in core[key]:
                    copy.wait_recv()

        def both_ways(h, dx):
            mine = piece(h, 0, dx)
            return move(mine, 1, 0, 0), move(mine, 3, 0, 0)

        far, crossed = {}, {}

        def cross(h, dy):
            crossed[h, dy] = move(piece(h, dy, 0), 0, 1, 0)

        def pass_on(h, dx, pair):
            pair[0].wait_recv()
            a = move(half(h, 0, 3, dx), 1, 0, 0)
            share(h, 3, dx)
            if h == 1:
                cross(h, 3)
            pair[1].wait_recv()
            b = move(half(h, 1, 1, dx), 3, 0, 0)
            share(h, 1, dx)
            if h == 1:
                cross(h, 1)
            far[h, dx] = (a, b)

        def end_far(h, dx):
            for copy in far[h, dx]:
                copy.wait_recv()
            share(h, 2, dx)
            if h == 1:
                cross(h, 2)

        def end_cross(dy):
            crossed[1, dy].wait_recv()
            share(1, dy, 1)

        wait_b(layer, 1)
        along1 = both_ways(1, 0)
        share(1, 0, 0)
        wait_b(layer, 0)
        cross(0, 0)
        along0 = both_ways(0, 0)
        share(0, 0, 0)
        cross(1, 0)
        ready((1, 0, 0), (0, 0, 0))
        products(layer, [(0, chip(0, 0)), (1, chip(0, 0))], out, every)
        pass_on(1, 0, along1)
        crossed[0, 0].wait_recv()
        along2 = both_ways(0, 1)
        share(0, 0, 1)
        pass_on(0, 0, along0)
        ready((1, 1, 0), (1, 3, 0))
        products(layer, [(1, chip(1, 0)), (1, chip(3, 0))], out, every)
        end_far(1, 0)
        end_cross(0)
        ready((0, 0, 1), (0, 3, 0))
        products(layer, [(0, chip(3, 0)), (0, chip(0, 1))], out, every)
        pass_on(0, 1, along2)
        ready((0, 1, 0), (1, 2, 0), (1, 0, 1))
        products(layer, [(0, chip(1, 0)), (1, chip(2, 0)), (1, chip(0, 1))], out, every)
        end_cross(1)
        end_cross(3)
        end_far(0, 0)
        ready((0, 1, 1), (0, 3, 1))
        products(layer, [(0, chip(1, 1)), (0, chip(3, 1))], out, every)
        end_cross(2)
        ready((1, 1, 1), (1, 3, 1), (0, 2, 0))
        products(layer, [(1, chip(1, 1)), (1, chip(3, 1)), (0, chip(2, 0))], out, every)
        end_far(0, 1)
        ready((1, 2, 1))
        products(layer, [(1, chip(2, 1))], out, every)
        ready((0, 2, 1))
        for h in range(2):
            products(
                layer, [(0, chip(2, 1))], out, rows_of[h], h == 0
            )
            begin[h]()

    class ZFirst:
        def __init__(self, part, buf, made):
            self.part, self.buf, self.made = part, buf, made

        def start(self):
            up, down = (row, reps_dev(0, 1)), (row, reps_dev(0, 3))
            part, buf = self.part, self.buf
            self.raw = [
                remote(part((z + 2) % 4), buf.at[0], up),
                remote(part(4 + (z + 2) % 4), buf.at[1], down),
            ]
            self.second = [
                remote(part(4 + (z + 1) % 4), buf.at[3], up),
                remote(part((z + 3) % 4), buf.at[4], down),
            ]

        def pass_on(self):
            up, down = (row, reps_dev(0, 1)), (row, reps_dev(0, 3))
            buf, made = self.buf, self.made
            self.raw[0].wait_recv()
            made[0] = self.part((z + 1) % 4)[...] + buf[0]
            self.second.append(remote(made.at[0], buf.at[2], up))
            self.raw[1].wait_recv()
            made[1] = self.part(4 + (z + 3) % 4)[...] + buf[1]
            self.second.append(remote(made.at[1], buf.at[5], down))

        def cross(self):
            for copy in self.second:
                copy.wait_recv()
            other, buf = 1 - xl, self.buf
            self.made[2] = self.part(other * 4 + z)[...] + buf[2 + other] + buf[4 + other]
            self.last = remote(self.made.at[2], buf.at[6], (row, reps_dev(1, 0)))

        def total(self):
            buf = self.buf
            mine = self.part(rep)[...] + buf[2 + xl] + buf[4 + xl]
            self.last.wait_recv()
            return mine + buf[6]

    class XFirst:
        def __init__(self, part, buf, made):
            self.part, self.buf, self.made = part, buf, made
            self.n = made.shape[1] // 2

        def start(self):
            over = (row, reps_dev(1, 0))
            self.over = {
                b: remote(self.part(reps_dev(1, b)), self.buf.at[b], over) for b in (2, 1, 3, 0)
            }

        def near(self, b):
            self.over[b].wait_recv()
            return self.part(reps_dev(0, b))[...] + self.buf[b]

        def halves(self, ref):
            return ref.at[pl.ds(0, self.n)], ref.at[pl.ds(self.n, self.n)]

        def send_far(self):
            up, down = (row, reps_dev(0, 1)), (row, reps_dev(0, 3))
            made, buf = self.made, self.buf
            made[0] = self.near(2)
            (m0, m1), (b0, b1) = self.halves(made.at[0]), self.halves(buf.at[4])
            self.far = [remote(m0, b0, up), remote(m1, b1, down)]

        def send_near(self):
            up, down = (row, reps_dev(0, 1)), (row, reps_dev(0, 3))
            made, buf = self.made, self.buf
            made[1] = self.near(1)
            self.up, self.up_to = self.halves(made.at[1]), self.halves(buf.at[5])
            self.last = [remote(self.up[1], self.up_to[1], up)]
            made[2] = self.near(3)
            self.down, self.down_to = self.halves(made.at[2]), self.halves(buf.at[6])
            self.last.append(remote(self.down[0], self.down_to[0], down))

        def pass_on(self):
            up, down = (row, reps_dev(0, 1)), (row, reps_dev(0, 3))
            n, made, buf = self.n, self.made, self.buf
            self.far[0].wait_recv()
            made[1, 0:n] += buf[4, 0:n]
            self.last.append(remote(self.up[0], self.up_to[0], up))
            self.far[1].wait_recv()
            made[2, n:] += buf[4, n:]
            self.last.append(remote(self.down[1], self.down_to[1], down))

        def total(self):
            mine = self.near(0)
            for copy in self.last:
                copy.wait_recv()
            return mine + self.buf[5] + self.buf[6]

    def transform(total, layer):
        wh, wl = w_high[layer], w_low[layer]
        th, tl = split(total.reshape(128, 256))
        return mm(th, wh) + mm(th, wl) + mm(tl, wh)

    def add_up(x_first, z_first, use):
        z_first.pass_on()
        x_first.send_far()
        z_first.cross()
        x_first.send_near()
        x_first.pass_on()
        use(1, z_first.total())
        use(0, x_first.total())

    send_a(0, lambda q, k: x_ref.at[:, pl.ds(2 * q, 2), k], near_peers)
    place_tiles()
    for layer in range(2):
        w_high[layer], w_low[layer] = split(w_ref[layer])
    hi[256] = jnp.zeros((128, 128), BF)
    lo[256] = jnp.zeros((128, 128), BF)

    def clear(i, carry):
        acc[i] = jnp.zeros((8, 8, 256), F32)
        acc_out[i] = jnp.zeros((8, 8, 256), F32)
        return carry

    lax.fori_loop(0, 32, clear, 0)
    convert(0, 4)
    fetch_plan.wait()
    turn(0, 0, ((1, 1), (0, 0)))
    convert(4, 256 // GROUP)
    pltpu.make_async_copy(pos_made, pos, pos_sem).wait()

    def mid_part(h):
        return lambda k: acc.at[pl.ds(16 * h, 16), k]

    def end_part(h):
        return lambda k: acc_out.at[pl.ds(4 * k + 2 * h, 2)]

    mid = XFirst(mid_part(0), mx, mx_made), ZFirst(mid_part(1), mz, mz_made)
    end = XFirst(end_part(0), ex, ex_made), ZFirst(end_part(1), ez, ez_made)

    gather_and_multiply(
        0, acc, (range(8), range(8, 16)), (mid[0].start, mid[1].start)
    )

    def use_mid(h, total):
        hid[h] = jnp.maximum(transform(total, 0), 0.0).reshape(16, 8, 256)
        send_a(
            1 + h,
            lambda q, k: hid.at[pl.ds(h, 1), pl.ds(2 * q, 2)],
            [(peer, rep) for peer in row_peers],
        )

    add_up(*mid, use_mid)
    turn(1, 2, ((0, 1),))
    turn(1, 1, ((0, 0),))
    gather_and_multiply(
        1, acc_out, (range(0, 16, 2), range(1, 16, 2)), (end[0].start, end[1].start)
    )

    def use_end(h, total):
        o_ref[128 * h : 128 * h + 128] = transform(total, 1)

    add_up(*end, use_end)

    for copy in sent:
        copy.wait_send()
    for n in range(3):
        some = big[n].at[0:7, 0]
        pltpu.make_async_copy(some, some, a_send.at[n]).wait()
    for layer in range(2):
        for h in range(2):
            some = send_b.at[layer, h, 0:7]
            pltpu.make_async_copy(some, some, b_send.at[layer, h]).wait()


def shards(features, adjacency_tiles, tile_rows, tile_cols, tile_counts, plan, weights):
    piece = (16, 8, 256)
    flat = (2, 8, 8, 256)
    dma = pltpu.SemaphoreType.DMA
    product = pl.pallas_call(
        kernel,
        name="graph_layers",
        out_shape=jax.ShapeDtypeStruct((256, 256), F32),
        in_specs=[
            pl.BlockSpec(memory_space=pltpu.VMEM),
            pl.BlockSpec(memory_space=pltpu.VMEM),
            pl.BlockSpec(memory_space=pltpu.SMEM),
            pl.BlockSpec(memory_space=pl.ANY),
            pl.BlockSpec(memory_space=pl.ANY),
            pl.BlockSpec(memory_space=pl.ANY),
            pl.BlockSpec(memory_space=pltpu.VMEM),
        ],
        out_specs=pl.BlockSpec(memory_space=pltpu.VMEM),
        scratch_shapes=[
            pltpu.VMEM((STAGES, GROUP, 128, 128), F32),
            pltpu.VMEM((257, 128, 128), BF),
            pltpu.VMEM((257, 128, 128), BF),
            pltpu.VMEM((2, 2, 2, 16, 8, 8, 256), F32),
            pltpu.VMEM((32, 8, 8, 256), F32),
            pltpu.VMEM((32, 8, 8, 256), F32),
            pltpu.VMEM((8, 2, 2, 2, 8, 256), F32),
            pltpu.VMEM((8, 2, 1, 2, 8, 256), F32),
            pltpu.VMEM((8, 2, 1, 2, 8, 256), F32),
            pltpu.VMEM((2, 2, 8, 2, 8, 256), F32),
            pltpu.VMEM((2, 16, 8, 256), F32),
            pltpu.VMEM((3, 256, 256), BF),
            pltpu.VMEM((3, 256, 256), BF),
            pltpu.VMEM((2, 256, 256), BF),
            pltpu.VMEM((2, 256, 256), BF),
            pltpu.VMEM((7,) + piece, F32),
            pltpu.VMEM((3,) + piece, F32),
            pltpu.VMEM((7,) + piece, F32),
            pltpu.VMEM((3,) + piece, F32),
            pltpu.VMEM((7,) + flat, F32),
            pltpu.VMEM((3,) + flat, F32),
            pltpu.VMEM((7,) + flat, F32),
            pltpu.VMEM((3,) + flat, F32),
            pltpu.VMEM((4, 128), jnp.int32),
            pltpu.SMEM((4, 128), jnp.int32),
            pltpu.SMEM((2, 8), jnp.int32),
            dma,
            dma,
            dma((STAGES,)),
            dma((COPIES,)),
            dma((COPIES,)),
            dma((3,)),
            dma((3,)),
            dma((2, 2)),
            dma((2, 2)),
        ],
        compiler_params=pltpu.CompilerParams(
            collective_id=0, has_side_effects=True, vmem_limit_bytes=58 * 2**20
        ),
    )(
        tile_rows.reshape(1, 256),
        tile_cols.reshape(1, 256),
        tile_counts,
        plan.T,
        features.reshape(2, 16, 8, 8, 256),
        adjacency_tiles.reshape(256, 128, 128),
        weights,
    )
    return jnp.maximum(product, 0.0)


def solution(mesh):
    return jax.shard_map(
        shards,
        mesh=mesh,
        in_specs=(
            P("row", None),
            P("row", "rep", None, None, None),
            P("row", "rep", None),
            P("row", "rep", None),
            P("row", "rep"),
            P(),
            P(),
        ),
        out_specs=P(("row", "rep"), None),
        check_vma=False,
    )
```

```python
import functools

import jax
import jax.numpy as jnp
from jax import lax
from jax.experimental import pallas as pl
from jax.experimental.pallas import tpu as pltpu
from jax.sharding import PartitionSpec as P

BF = jnp.bfloat16
F32 = jnp.float32
MESH = pl.DeviceIdType.MESH
Y, XH, C, XL, Z = 4, 2, 2, 2, 4
GROUP = 16
STAGES = 4
COPIES = 160


def mm(a, b):
    return jnp.dot(a, b, preferred_element_type=F32)


def split(v):
    high = v.astype(BF)
    return high, (v - high.astype(F32)).astype(BF)


def kernel(
    rows_ref, cols_ref, count_ref, plan_ref, x_ref, tiles, w_ref, o_ref,
    stage, hi, lo, land, acc, acc_out, big_0, big_10, big_11, send_b, hid, bh, bl, w_high, w_low,
    mx, mx_made, mz, mz_made, ex, ex_made, ez, ez_made,
    pos_made, pos, plan, pos_sem, plan_sem, stage_sem, ssem, rsem, a_send, a_recv, b_send, b_recv,
):
    row, rep = lax.axis_index("row"), lax.axis_index("rep")
    y, xh, c = row // 4, (row // 2) % 2, row % 2
    xl, z = rep // 4, rep % 4

    def rows_dev(dy, dx, dc):
        return ((y + dy) % 4) * 4 + ((xh + dx) % 2) * 2 + (c + dc) % 2

    def reps_dev(dx, dz):
        return ((xl + dx) % 2) * 4 + (z + dz) % 4

    plane = [(2, 1), (2, 0), (1, 1), (3, 1), (0, 1), (1, 0), (3, 0)]
    row_peers = [rows_dev(a, b, 0) for a, b in plane]
    near_peers = [(rows_dev(a, b, 0), reps_dev(b, 0)) for a, b in plane]
    rep_peers = [
        reps_dev(a, b) for a, b in ((1, 2), (0, 2), (1, 1), (1, 3), (1, 0), (0, 1), (0, 3))
    ]

    def load_tiles(g, slot):
        return pltpu.make_async_copy(
            tiles.at[pl.ds(g * GROUP, GROUP)], stage.at[slot], stage_sem.at[slot]
        )

    for g in range(STAGES):
        load_tiles(g, g).start()

    fetch_plan = pltpu.make_async_copy(plan_ref, plan, plan_sem)
    fetch_plan.start()
    barrier = pltpu.get_barrier_semaphore()
    for peer in row_peers + [rows_dev(0, 0, 1)]:
        pl.semaphore_signal(barrier, inc=1, device_id=(peer, rep), device_id_type=MESH)
    for peer in rep_peers:
        pl.semaphore_signal(barrier, inc=1, device_id=(row, peer), device_id_type=MESH)
    for (_, b), (peer, to) in zip(plane, near_peers):
        if b:
            pl.semaphore_signal(barrier, inc=1, device_id=(peer, to), device_id_type=MESH)
    pl.semaphore_wait(barrier, 19)

    used = [0]
    sent = []

    def remote(src, dst, dev):
        n = used[0]
        used[0] += 1
        copy = pltpu.make_async_remote_copy(
            src_ref=src, dst_ref=dst, send_sem=ssem.at[n], recv_sem=rsem.at[n],
            device_id=dev, device_id_type=MESH,
        )
        sent.append(copy)
        copy.start()
        return copy

    big = (big_0, big_10, big_11)
    here = row // 2

    def send_a(n, source, peers):
        for peer, to in peers:
            pltpu.make_async_remote_copy(
                src_ref=source(peer // 2, to), dst_ref=big[n].at[here, c],
                send_sem=a_send.at[n], recv_sem=a_recv.at[n],
                device_id=(peer, to), device_id_type=MESH,
            ).start()
        pltpu.make_async_copy(source(here, rep), big[n].at[here, c], a_recv.at[n]).start()

    def turn(layer, n, chunks):
        plane_part = big[n].at[:, c]
        pltpu.make_async_copy(plane_part, plane_part, a_recv.at[n]).wait()
        other = big[n].at[:, c, :, 1 - c]
        remote(other, other, (rows_dev(0, 0, 1), rep)).wait_recv()
        for at, h in chunks:
            for k in range(8):
                for s in range(2):
                    r = plan[s, k]
                    send_b[layer, h, k, s] = big[n][r // 2, r % 2, at, c]
            for peer in rep_peers:
                pltpu.make_async_remote_copy(
                    src_ref=send_b.at[layer, h, peer], dst_ref=land.at[layer, :, h, row, rep],
                    send_sem=b_send.at[layer, h], recv_sem=b_recv.at[layer, h],
                    device_id=(row, peer), device_id_type=MESH,
                ).start()
            pltpu.make_async_copy(
                send_b.at[layer, h, rep], land.at[layer, :, h, row, rep], b_recv.at[layer, h]
            ).start()

    def wait_b(layer, h):
        mine = land.at[layer, :, h, row]
        pltpu.make_async_copy(mine, mine, b_recv.at[layer, h]).wait()

    def place_tiles():
        slot = lax.broadcasted_iota(jnp.int32, (1, 256), 1)
        key = jnp.where(slot < count_ref[0, 0], rows_ref[...] * 32 + cols_ref[...], -1)
        down = lax.broadcasted_iota(jnp.int32, (128, 128), 0)
        spot = lax.broadcasted_iota(jnp.int32, (128, 128), 1)
        keys = [
            jnp.broadcast_to(key[:, 128 * n : 128 * n + 128], (128, 128)).T for n in range(2)
        ]
        for b in range(4):
            found = jnp.minimum(
                jnp.where(keys[0] == spot + 128 * b, down, 256),
                jnp.where(keys[1] == spot + 128 * b, down + 128, 256),
            )
            pos_made[b : b + 1] = jnp.min(found, axis=0, keepdims=True)
        pltpu.make_async_copy(pos_made, pos, pos_sem).start()

    def convert(first, last):
        def one(g, carry):
            slot = lax.rem(g, STAGES)
            load_tiles(g, slot).wait()

            def tile(t, inner):
                high, low = split(stage[slot, t])
                hi[g * GROUP + t] = high
                lo[g * GROUP + t] = low
                return inner

            lax.fori_loop(0, GROUP, tile, 0, unroll=4)

            @pl.when(g + STAGES < 256 // GROUP)
            def _():
                load_tiles(g + STAGES, slot).start()

            return carry

        lax.fori_loop(first, last, one, 0)

    def products(layer, chips, out, row_tiles, fresh=True):
        right = []
        for n, (h, q) in enumerate(chips):
            if fresh:
                for s in range(2):
                    part = land[layer, s, h, pl.ds(q * 2, 2)].reshape(128, 256)
                    r = slice(128 * s, 128 * s + 128)
                    bh[n, r], bl[n, r] = split(part)
            right += [bh[n], bh[n], bl[n]]
        right = jnp.concatenate(right, axis=0)
        for i in row_tiles:
            left = []
            for h, q in chips:
                t = h * 8 + q
                a0, a1 = pos[i // 4, i % 4 * 32 + t], pos[i // 4, i % 4 * 32 + 16 + t]
                top0, top1 = hi[a0], hi[a1]
                left += [top0, top1, lo[a0], lo[a1], top0, top1]
            added = mm(jnp.concatenate(left, axis=1), right)
            out[2 * i : 2 * i + 2] += added.reshape(2, 8, 8, 256)

    def chip(dy, dx):
        return ((y + dy) % 4) * 2 + (xh + dx) % 2

    def gather_and_multiply(layer, out, rows_of, begin):
        every = range(16)
        core = {}

        def piece(h, dy, dx):
            return land.at[layer, :, h, chip(dy, dx) * 2 + c]

        def half(h, s, dy, dx):
            return land.at[layer, s, h, chip(dy, dx) * 2 + c]

        def move(ref, dy, dx, dc):
            return remote(ref, ref, (rows_dev(dy, dx, dc), rep))

        def share(h, dy, dx):
            core.setdefault((h, dy, dx), []).append(move(piece(h, dy, dx), 0, 0, 1))

        def ready(*keys):
            for key in keys:
                for copy in core[key]:
                    copy.wait_recv()

        def both_ways(h, dx):
            mine = piece(h, 0, dx)
            return move(mine, 1, 0, 0), move(mine, 3, 0, 0)

        far, crossed = {}, {}

        def cross(h, dy):
            crossed[h, dy] = move(piece(h, dy, 0), 0, 1, 0)

        def pass_on(h, dx, pair):
            pair[0].wait_recv()
            a = move(half(h, 0, 3, dx), 1, 0, 0)
            share(h, 3, dx)
            if h == 1:
                cross(h, 3)
            pair[1].wait_recv()
            b = move(half(h, 1, 1, dx), 3, 0, 0)
            share(h, 1, dx)
            if h == 1:
                cross(h, 1)
            far[h, dx] = (a, b)

        def end_far(h, dx):
            for copy in far[h, dx]:
                copy.wait_recv()
            share(h, 2, dx)
            if h == 1:
                cross(h, 2)

        def end_cross(dy):
            crossed[1, dy].wait_recv()
            share(1, dy, 1)

        wait_b(layer, 1)
        along1 = both_ways(1, 0)
        share(1, 0, 0)
        wait_b(layer, 0)
        cross(0, 0)
        along0 = both_ways(0, 0)
        share(0, 0, 0)
        cross(1, 0)
        ready((1, 0, 0), (0, 0, 0))
        products(layer, [(0, chip(0, 0)), (1, chip(0, 0))], out, every)
        pass_on(1, 0, along1)
        crossed[0, 0].wait_recv()
        along2 = both_ways(0, 1)
        share(0, 0, 1)
        pass_on(0, 0, along0)
        ready((1, 1, 0), (1, 3, 0))
        products(layer, [(1, chip(1, 0)), (1, chip(3, 0))], out, every)
        end_far(1, 0)
        end_cross(0)
        ready((0, 0, 1), (0, 3, 0))
        products(layer, [(0, chip(3, 0)), (0, chip(0, 1))], out, every)
        pass_on(0, 1, along2)
        ready((0, 1, 0), (1, 2, 0), (1, 0, 1))
        products(layer, [(0, chip(1, 0)), (1, chip(2, 0)), (1, chip(0, 1))], out, every)
        end_cross(1)
        end_cross(3)
        end_far(0, 0)
        ready((0, 1, 1), (0, 3, 1))
        products(layer, [(0, chip(1, 1)), (0, chip(3, 1))], out, every)
        end_cross(2)
        ready((1, 1, 1), (1, 3, 1), (0, 2, 0))
        products(layer, [(1, chip(1, 1)), (1, chip(3, 1)), (0, chip(2, 0))], out, every)
        end_far(0, 1)
        ready((1, 2, 1))
        products(layer, [(1, chip(2, 1))], out, every)
        ready((0, 2, 1))
        for h in range(2):
            products(
                layer, [(0, chip(2, 1))], out, rows_of[h], h == 0
            )
            begin[h]()

    class ZFirst:
        def __init__(self, part, buf, made):
            self.part, self.buf, self.made = part, buf, made

        def start(self):
            up, down = (row, reps_dev(0, 1)), (row, reps_dev(0, 3))
            part, buf = self.part, self.buf
            self.raw = [
                remote(part((z + 2) % 4), buf.at[0], up),
                remote(part(4 + (z + 2) % 4), buf.at[1], down),
            ]
            self.second = [
                remote(part(4 + (z + 1) % 4), buf.at[3], up),
                remote(part((z + 3) % 4), buf.at[4], down),
            ]

        def pass_on(self):
            up, down = (row, reps_dev(0, 1)), (row, reps_dev(0, 3))
            buf, made = self.buf, self.made
            self.raw[0].wait_recv()
            made[0] = self.part((z + 1) % 4)[...] + buf[0]
            self.second.append(remote(made.at[0], buf.at[2], up))
            self.raw[1].wait_recv()
            made[1] = self.part(4 + (z + 3) % 4)[...] + buf[1]
            self.second.append(remote(made.at[1], buf.at[5], down))

        def cross(self):
            for copy in self.second:
                copy.wait_recv()
            other, buf = 1 - xl, self.buf
            self.made[2] = self.part(other * 4 + z)[...] + buf[2 + other] + buf[4 + other]
            self.last = remote(self.made.at[2], buf.at[6], (row, reps_dev(1, 0)))

        def total(self):
            buf = self.buf
            mine = self.part(rep)[...] + buf[2 + xl] + buf[4 + xl]
            self.last.wait_recv()
            return mine + buf[6]

    class XFirst:
        def __init__(self, part, buf, made):
            self.part, self.buf, self.made = part, buf, made
            self.n = made.shape[1] // 2

        def start(self):
            over = (row, reps_dev(1, 0))
            self.over = {
                b: remote(self.part(reps_dev(1, b)), self.buf.at[b], over) for b in (2, 1, 3)
            }

        def start_last(self):
            over = (row, reps_dev(1, 0))
            self.over[0] = remote(self.part(reps_dev(1, 0)), self.buf.at[0], over)

        def near(self, b):
            self.over[b].wait_recv()
            return self.part(reps_dev(0, b))[...] + self.buf[b]

        def halves(self, ref):
            return ref.at[pl.ds(0, self.n)], ref.at[pl.ds(self.n, self.n)]

        def send_far(self):
            up, down = (row, reps_dev(0, 1)), (row, reps_dev(0, 3))
            made, buf = self.made, self.buf
            made[0] = self.near(2)
            (m0, m1), (b0, b1) = self.halves(made.at[0]), self.halves(buf.at[4])
            self.far = [remote(m0, b0, up), remote(m1, b1, down)]

        def send_near(self):
            up, down = (row, reps_dev(0, 1)), (row, reps_dev(0, 3))
            made, buf = self.made, self.buf
            made[1] = self.near(1)
            self.up, self.up_to = self.halves(made.at[1]), self.halves(buf.at[5])
            self.last = [remote(self.up[1], self.up_to[1], up)]
            made[2] = self.near(3)
            self.down, self.down_to = self.halves(made.at[2]), self.halves(buf.at[6])
            self.last.append(remote(self.down[0], self.down_to[0], down))

        def pass_on(self):
            up, down = (row, reps_dev(0, 1)), (row, reps_dev(0, 3))
            n, made, buf = self.n, self.made, self.buf
            self.far[0].wait_recv()
            made[1, 0:n] += buf[4, 0:n]
            self.last.append(remote(self.up[0], self.up_to[0], up))
            self.far[1].wait_recv()
            made[2, n:] += buf[4, n:]
            self.last.append(remote(self.down[1], self.down_to[1], down))

        def total(self):
            mine = self.near(0)
            for copy in self.last:
                copy.wait_recv()
            return mine + self.buf[5] + self.buf[6]

    def transform(total, layer):
        wh, wl = w_high[layer], w_low[layer]
        th, tl = split(total.reshape(128, 256))
        return mm(th, wh) + mm(th, wl) + mm(tl, wh)

    def add_up(x_first, z_first, use):
        z_first.pass_on()
        x_first.send_far()
        x_first.start_last()
        z_first.cross()
        x_first.send_near()
        x_first.pass_on()
        use(1, z_first.total())
        use(0, x_first.total())

    send_a(0, lambda q, k: x_ref.at[:, pl.ds(2 * q, 2), k], near_peers)
    place_tiles()
    for layer in range(2):
        w_high[layer], w_low[layer] = split(w_ref[layer])
    hi[256] = jnp.zeros((128, 128), BF)
    lo[256] = jnp.zeros((128, 128), BF)

    def clear(i, carry):
        acc[i] = jnp.zeros((8, 8, 256), F32)
        acc_out[i] = jnp.zeros((8, 8, 256), F32)
        return carry

    lax.fori_loop(0, 32, clear, 0)
    convert(0, 4)
    fetch_plan.wait()
    turn(0, 0, ((1, 1), (0, 0)))
    convert(4, 256 // GROUP)
    pltpu.make_async_copy(pos_made, pos, pos_sem).wait()

    def mid_part(h):
        return lambda k: acc.at[pl.ds(16 * h, 16), k]

    def end_part(h):
        return lambda k: acc_out.at[pl.ds(4 * k + 2 * h, 2)]

    mid = XFirst(mid_part(0), mx, mx_made), ZFirst(mid_part(1), mz, mz_made)
    end = XFirst(end_part(0), ex, ex_made), ZFirst(end_part(1), ez, ez_made)

    gather_and_multiply(
        0, acc, (range(8), range(8, 16)), (mid[0].start, mid[1].start)
    )

    def use_mid(h, total):
        hid[h] = jnp.maximum(transform(total, 0), 0.0).reshape(16, 8, 256)
        send_a(
            1 + h,
            lambda q, k: hid.at[pl.ds(h, 1), pl.ds(2 * q, 2)],
            [(peer, rep) for peer in row_peers],
        )

    add_up(*mid, use_mid)
    turn(1, 2, ((0, 1),))
    turn(1, 1, ((0, 0),))
    gather_and_multiply(
        1, acc_out, (range(0, 16, 2), range(1, 16, 2)), (end[0].start, end[1].start)
    )

    def use_end(h, total):
        o_ref[128 * h : 128 * h + 128] = transform(total, 1)

    add_up(*end, use_end)

    for copy in sent:
        copy.wait_send()
    for n in range(3):
        some = big[n].at[0:7, 0]
        pltpu.make_async_copy(some, some, a_send.at[n]).wait()
    for layer in range(2):
        for h in range(2):
            some = send_b.at[layer, h, 0:7]
            pltpu.make_async_copy(some, some, b_send.at[layer, h]).wait()


def shards(features, adjacency_tiles, tile_rows, tile_cols, tile_counts, plan, weights):
    piece = (16, 8, 256)
    flat = (2, 8, 8, 256)
    dma = pltpu.SemaphoreType.DMA
    product = pl.pallas_call(
        kernel,
        name="graph_layers",
        out_shape=jax.ShapeDtypeStruct((256, 256), F32),
        in_specs=[
            pl.BlockSpec(memory_space=pltpu.VMEM),
            pl.BlockSpec(memory_space=pltpu.VMEM),
            pl.BlockSpec(memory_space=pltpu.SMEM),
            pl.BlockSpec(memory_space=pl.ANY),
            pl.BlockSpec(memory_space=pl.ANY),
            pl.BlockSpec(memory_space=pl.ANY),
            pl.BlockSpec(memory_space=pltpu.VMEM),
        ],
        out_specs=pl.BlockSpec(memory_space=pltpu.VMEM),
        scratch_shapes=[
            pltpu.VMEM((STAGES, GROUP, 128, 128), F32),
            pltpu.VMEM((257, 128, 128), BF),
            pltpu.VMEM((257, 128, 128), BF),
            pltpu.VMEM((2, 2, 2, 16, 8, 8, 256), F32),
            pltpu.VMEM((32, 8, 8, 256), F32),
            pltpu.VMEM((32, 8, 8, 256), F32),
            pltpu.VMEM((8, 2, 2, 2, 8, 256), F32),
            pltpu.VMEM((8, 2, 1, 2, 8, 256), F32),
            pltpu.VMEM((8, 2, 1, 2, 8, 256), F32),
            pltpu.VMEM((2, 2, 8, 2, 8, 256), F32),
            pltpu.VMEM((2, 16, 8, 256), F32),
            pltpu.VMEM((3, 256, 256), BF),
            pltpu.VMEM((3, 256, 256), BF),
            pltpu.VMEM((2, 256, 256), BF),
            pltpu.VMEM((2, 256, 256), BF),
            pltpu.VMEM((7,) + piece, F32),
            pltpu.VMEM((3,) + piece, F32),
            pltpu.VMEM((7,) + piece, F32),
            pltpu.VMEM((3,) + piece, F32),
            pltpu.VMEM((7,) + flat, F32),
            pltpu.VMEM((3,) + flat, F32),
            pltpu.VMEM((7,) + flat, F32),
            pltpu.VMEM((3,) + flat, F32),
            pltpu.VMEM((4, 128), jnp.int32),
            pltpu.SMEM((4, 128), jnp.int32),
            pltpu.SMEM((2, 8), jnp.int32),
            dma,
            dma,
            dma((STAGES,)),
            dma((COPIES,)),
            dma((COPIES,)),
            dma((3,)),
            dma((3,)),
            dma((2, 2)),
            dma((2, 2)),
        ],
        compiler_params=pltpu.CompilerParams(
            collective_id=0, has_side_effects=True, vmem_limit_bytes=58 * 2**20
        ),
    )(
        tile_rows.reshape(1, 256),
        tile_cols.reshape(1, 256),
        tile_counts,
        plan.T,
        features.reshape(2, 16, 8, 8, 256),
        adjacency_tiles.reshape(256, 128, 128),
        weights,
    )
    return jnp.maximum(product, 0.0)


def solution(mesh):
    return jax.shard_map(
        shards,
        mesh=mesh,
        in_specs=(
            P("row", None),
            P("row", "rep", None, None, None),
            P("row", "rep", None),
            P("row", "rep", None),
            P("row", "rep"),
            P(),
            P(),
        ),
        out_specs=P(("row", "rep"), None),
        check_vma=False,
    )
```
